128 devices in a mesh: node: 16 (over y, z), local: 8 (over x, core).
Axes of the slice: x: 4, y: 4, z: 4, core: 2. Of those that a mesh axis runs over, the one named last changes fastest.
Arguments:
- tokens: bfloat16 [512, 7168], P(('node', 'local')), may hold values from -6 to 6
- expert_ids: int32 [512, 8], P(('node', 'local')), may hold values from 0 to 31, all different within a row; in each aligned block of 4 rows (0 to 3, 4 to 7, ...) at most 3 rows name the same one
- route_weights: float32 [512, 8], P(('node', 'local')), may hold values from 0.1 to 0.6
- w_gate: bfloat16 [32, 7168, 2048], P('node', None, 'local'), may hold values from -0.0625 to 0.0625
- w_up: bfloat16 [32, 7168, 2048], P('node', None, 'local'), may hold values from -0.0625 to 0.0625
- w_down: bfloat16 [32, 2048, 7168], P('node', 'local'), may hold values from -0.125 to 0.125
Outputs:
- mixed: bfloat16 [512, 7168], P(('node', 'local'))
The draws below stay inside these ranges and needn't reach their ends.
Inputs may be any that keep to these rules, and one draw needn't show every extreme that they name: `expert_ids`: each row names 8 different experts. Among the rows of one device no expert is named by more than 3 rows, and in every draw some expert is named by exactly 3 rows of some device.
All inputs are finite; a program needn't handle non-finite values.
Results may differ from the reference program's by a relative error of at most 0.0049.
Values may be sent and summed in bfloat16 or wider, within the bound.
A program may use at most 192 MiB of HBM per device.

```python
import math
import jax
import jax.numpy as jnp
import numpy as np
from jax import lax

D = 7168
FF = 2048
TOP = 8
TOK_DEV = 4
CAP = 3
EXPERTS = 32
TOKENS = 512
N_NODE = 16
N_LOCAL = 8


def shard_levels(key, shape, cuts, smallest, largest):
    level, own = 1.0, jax.random.fold_in(key, 6)
    for axis_at, parts in cuts:
        draws = jnp.exp(jax.random.uniform(jax.random.fold_in(own, axis_at), (parts,), jnp.float32, smallest / len(cuts), largest / len(cuts)))
        level = level * jnp.repeat(draws, shape[axis_at] // parts).reshape([-1 if axis == axis_at else 1 for axis in range(len(shape))])
    return level


def routed_block(rng, own, number, rows, count, top, bound, skew):
    ranking = jax.random.permutation(rng, count)
    heavy_load, common = portions_of(count, rows * top, bound, skew, True), portions_of(count, rows * top, bound, skew, False)
    places = jnp.arange(count)

    def named(tallies, turn):
        used = int((tallies > 0).sum())
        fixed = max(1, used // 4)
        moved = fixed + (places - fixed + turn * (used - fixed)) % max(1, count - fixed)
        return jnp.zeros((count,), jnp.int32).at[ranking[jnp.where(places < fixed, places, moved)]].set(jnp.asarray(tallies, jnp.int32))

    tallies = jnp.where(number % 4 == 0, named(heavy_load, number // 4), named(common, number - number // 4 - 1))
    mixed = jax.random.permutation(jax.random.fold_in(own, 3), count)
    donor, taker = mixed[0:count // 2 * 2:2], mixed[1:count // 2 * 2:2]
    room = jnp.minimum(tallies[donor] - 1, bound - tallies[taker]) // 2
    room = jnp.where((donor == ranking[0]) | (taker == ranking[0]) | (tallies[taker] == 0), 0, jnp.maximum(room, 0))
    moved = jax.random.randint(jax.random.fold_in(own, 4), (count // 2,), 0, 1 << 20) % (room + 1)
    tallies = tallies.at[donor].add(-moved).at[taker].add(moved)
    items = jnp.searchsorted(jnp.cumsum(tallies), jnp.arange(rows * top), side="right").astype(jnp.int32)
    table = items.reshape(top, rows).T
    table = table[jax.random.permutation(jax.random.fold_in(own, 1), rows)]
    turn = jax.random.randint(jax.random.fold_in(own, 2), (rows, 1), 0, top)
    return jnp.take_along_axis(table, (jnp.arange(top)[None, :] + turn) % top, axis=1)


def portions_of(count, total, reach, lean, full):
    weights = [(1 << 20) // math.isqrt(rank ** lean) + 1 for rank in range(1, count + 1)]
    largest = reach if full else min(reach, max(-(-total // count), total * weights[0] // sum(weights)))
    least = 1 if total - largest >= count - 1 else 0
    given, surplus = [largest] + [least] * (count - 1), total - largest - least * (count - 1)
    while surplus > 0:
        free = [i for i in range(1, count) if given[i] < largest] or [i for i in range(1, count) if given[i] < reach]
        pool, left = sum([weights[i] for i in free]), surplus
        for i in free:
            extra = min(reach - given[i], max(1, left * weights[i] // pool), surplus)
            given[i] = given[i] + extra
            surplus = surplus - extra
    return np.array(given)


def centred(rng, dims, width, most, pieces=(), held_as=jnp.bfloat16):
    entries = jax.random.normal(rng, dims, jnp.float32) * width
    if len(pieces) > 0:
        entries = shard_levels(rng, dims, pieces, -0.22, 0.18) * entries
    return jnp.clip(entries, min=-most, max=most).astype(held_as)


def setup_inputs(seed: int = 0) -> dict:
    streams_of = jax.random.split(jax.random.key(seed), 7)
    tokens = centred(streams_of[0], (TOKENS, D), 1.0, 6.0, ((0, 128),))
    expert_ids_keys = jax.random.split(jax.random.fold_in(streams_of[1], 1), TOKENS // TOK_DEV)
    expert_ids_turns = jax.random.permutation(jax.random.fold_in(streams_of[1], 3), TOKENS // TOK_DEV)
    expert_ids = jax.vmap(lambda own, number: routed_block(jax.random.fold_in(streams_of[1], 2), own, number, TOK_DEV, EXPERTS, TOP, CAP, 2))(expert_ids_keys, expert_ids_turns).reshape((TOKENS, TOP))
    route_weights = jnp.clip(0.1 + 0.5 * jax.random.uniform(streams_of[2], (TOKENS, TOP), jnp.float32) ** shard_levels(streams_of[2], (TOKENS, TOP), ((0, 128),), -0.2, 0.2), 0.1, 0.6)
    w_gate = centred(streams_of[3], (EXPERTS, D, FF), D ** -0.5, 0.0625, ((0, 16), (2, 8)))
    w_up = centred(streams_of[4], (EXPERTS, D, FF), D ** -0.5, 0.0625, ((0, 16), (2, 8)))
    w_down = centred(streams_of[5], (EXPERTS, FF, D), FF ** -0.5, 0.125, ((0, 16), (1, 8)))
    return dict(tokens=tokens, expert_ids=expert_ids, route_weights=route_weights, w_gate=w_gate, w_up=w_up, w_down=w_down)


def reference(tokens, expert_ids, route_weights, w_gate, w_up, w_down):
    slot_count = N_NODE * N_LOCAL * CAP
    token_f32 = tokens.astype(jnp.float32)

    def add_expert(running, expert):
        naming = expert_ids == expert
        weight = jnp.sum(jnp.where(naming, route_weights, 0.0), axis=1)
        present = jnp.any(naming, axis=1)
        picked = jnp.nonzero(present, size=slot_count, fill_value=0)[0].astype(jnp.int32)
        amount = jnp.sum(present.astype(jnp.int32))
        in_range = jnp.arange(slot_count, dtype=jnp.int32) < amount
        chosen = token_f32[picked]
        gate_act = jnp.dot(chosen, w_gate[expert].astype(jnp.float32))
        up_act = jnp.dot(chosen, w_up[expert].astype(jnp.float32))
        hidden = (jax.nn.silu(gate_act) * up_act).astype(jnp.bfloat16).astype(jnp.float32)
        expert_out = jnp.dot(hidden, w_down[expert].astype(jnp.float32))
        row_scale = jnp.where(in_range, weight[picked], 0.0)
        running = running.at[picked].add(expert_out * row_scale[:, None])
        return running, None

    start_sum = jnp.zeros((TOKENS, D), jnp.float32)
    running, _ = lax.scan(add_expert, start_sum, jnp.arange(EXPERTS, dtype=jnp.int32))
    return running.astype(jnp.bfloat16)
```

```python
import jax
import jax.numpy as jnp
from jax import lax
from jax.experimental import pallas as pl
from jax.experimental.pallas import tpu as pltpu
from jax.sharding import PartitionSpec as P

MESH = pl.DeviceIdType.MESH
F32, BF16 = jnp.float32, jnp.bfloat16
LANE = 128
HALF = 3584
QUARTER = 1792
TOKENS = 512
WIDE = 640
ORDERS = ("xyz", "yzx", "zxy")
PLACE = {"z": 0, "y": 1, "x": 2}
FORWARD, BACK, FAR = 1, 3, 2
CHUNKS = {"A": (0, 6, (0, 256)), "B": (6, 6, (256, 256)), "C": (12, 2, (512, 128))}
N_SEMS = 240


def coordinates():
    node, local = lax.axis_index("node"), lax.axis_index("local")
    return {"x": local // 2, "y": node // 4, "z": node % 4, "core": local % 2}


def neighbour(axis, step):
    at = coordinates()
    if axis == "core":
        at["core"] = 1 - at["core"]
    else:
        at[axis] = lax.rem(at[axis] + step, 4)
    return (at["y"] * 4 + at["z"], at["x"] * 2 + at["core"])


def place(split, c=slice(None), b=slice(None), a=slice(None)):
    order = ORDERS[split]
    index = [None, None, None]
    for axis, value in zip(order, (a, b, c)):
        index[PLACE[axis]] = value
    return tuple(index)


def plane(split, b=slice(None), a=slice(None)):
    order = ORDERS[split]
    return tuple(v for _, v in sorted([(PLACE[order[0]], a), (PLACE[order[1]], b)], key=lambda p: p[0]))


def tiles_of(chunk, split):
    first, count, _ = CHUNKS[chunk]
    if chunk == "C":
        return (first + split, 1) if split < 2 else None
    return (first + 2 * split, 2)


def kernel(tokens, ids, weights, w_gate, w_up, w_down, out,
           own, sent, got, xs, lhs_a, lhs_b, lhs_c, wgu_a, wgu_b, wgu_c, wd, acc, hid, scale,
           own_sum, other_sum, core_got, r1, r2, r3, r4, fin, fin_got, send_sem, recv_sem, local_sem):
    core = lax.axis_index("local") % 2
    node = lax.axis_index("node")
    used = [0]
    pending = []

    def send(src, dst, axis, step=0):
        i = used[0]
        used[0] += 1
        copy = pltpu.make_async_remote_copy(
            src_ref=src, dst_ref=dst, send_sem=send_sem.at[i], recv_sem=recv_sem.at[i],
            device_id=neighbour(axis, step), device_id_type=MESH)
        copy.start()
        pending.append(copy)
        return copy

    barrier = pltpu.get_barrier_semaphore()
    friends = [(axis, step) for axis in "xyz" for step in (1, 2, 3)] + [("core", 0)]
    for axis, step in friends:
        pl.semaphore_signal(barrier, inc=1, device_id=neighbour(axis, step), device_id_type=MESH)

    fetches = {"A": [], "B": [], "C": [], "D": []}

    def fetch(src, dst, name):
        copy = pltpu.make_async_copy(src, dst, local_sem.at[sum(len(v) for v in fetches.values())])
        copy.start()
        fetches[name].append(copy)

    wgu = {"A": wgu_a, "B": wgu_b, "C": wgu_c}
    lhs = {"A": lhs_a, "B": lhs_b, "C": lhs_c}

    def fetch_chunk(name):
        first, count, _ = CHUNKS[name]
        for which, source in enumerate((w_gate, w_up)):
            for half in range(2):
                side = lax.rem(core + half, 2)
                for h in range(2):
                    start = pl.multiple_of(side * HALF + h * QUARTER + first * LANE, LANE)
                    fetch(source.at[:, pl.ds(start, count * LANE), :],
                          wgu[name].at[2 * which:2 * which + 2, pl.ds((half * 2 + h) * count * LANE, count * LANE), :], name)

    fetch_chunk("A")

    row4 = lax.broadcasted_iota(jnp.int32, (4, LANE), 1)
    dense = jnp.zeros((4, LANE), F32)
    for k in range(8):
        dense = dense + jnp.where(row4 % 32 == ids[:, k:k + 1], weights[:, k:k + 1], 0.0)
    high = dense.astype(BF16).astype(F32)
    mid = (dense - high).astype(BF16).astype(F32)
    low = dense - high - mid
    meta = jnp.where(row4 < 32, high, jnp.where(row4 < 64, mid, jnp.where(row4 < 96, low, 0.0)))
    left = tokens[:, :HALF].astype(F32)
    right = tokens[:, HALF:].astype(F32)
    mine = jnp.where(core == 0, left, right)
    theirs = jnp.where(core == 0, right, left)
    for r in (0, 4):
        own[r:r + 4, :HALF] = mine
        own[r:r + 4, HALF:] = meta
        sent[r:r + 4, :HALF] = theirs
        sent[r:r + 4, HALF:] = meta

    pl.semaphore_wait(barrier, len(friends))

    swap = send(sent, got, "core")
    fetch_chunk("B")
    swap.wait_recv()
    block = jnp.where(lax.broadcasted_iota(jnp.int32, (8, HALF + LANE), 0) // 4 == core, own[...], got[...])
    for split in range(3):
        for name, (_, _, (at, width)) in CHUNKS.items():
            span = tiles_of(name, split)
            if span is None:
                piece = jnp.concatenate([block[:, HALF:], block[:, HALF:]], axis=0)
            else:
                lo = span[0] * LANE
                piece = jnp.concatenate([block[:, lo:lo + width], block[:, QUARTER + lo:QUARTER + lo + width]], axis=0)
            xs[0, split, 0, 0, 0, :, at:at + width] = piece.astype(BF16)

    def xref(half, split, c, b=slice(None), a=slice(None), cols=None):
        index = (half, split) + place(split, c, b, a)
        if cols is not None:
            index = index + (slice(None), pl.ds(*cols))
        return xs.at[index]

    first, second = {}, {}
    for split in range(3):
        axis = ORDERS[split][0]
        first[split] = [send(xref(0, split, 0, 0, 0), xref(0, split, 0, 0, (4 - step) % 4), axis, step) for step in (1, 3, 2)]
    fetch_chunk("C")
    for half in range(2):
        side = lax.rem(core + half, 2)
        fetch(w_down.at[:, :, pl.ds(pl.multiple_of(side * HALF, LANE), HALF)], wd.at[half], "D")
    for split in range(3):
        axis = ORDERS[split][1]
        for copy in first[split]:
            copy.wait_recv()
        second[split] = [send(xref(0, split, 0, 0), xref(0, split, 0, (4 - step) % 4), axis, step) for step in (1, 3, 2)]

    third, passed, crossed = {}, {}, {}

    def spread(name, split):
        cols = CHUNKS[name][2]
        axis = ORDERS[split][2]
        third[name, split] = (
            send(xref(0, split, 0, cols=cols), xref(0, split, BACK, cols=cols), axis, 1),
            send(xref(0, split, 0, cols=cols), xref(0, split, FORWARD, cols=cols), axis, 3))

    def pass_on(name, split):
        cols = CHUNKS[name][2]
        axis = ORDERS[split][2]
        lower, upper = slice(0, 2), slice(2, 4)
        from_back, from_forward = third[name, split]
        from_back.wait_recv()
        one = send(xref(0, split, BACK, lower, cols=cols), xref(0, split, FAR, lower, cols=cols), axis, 1)
        from_forward.wait_recv()
        two = send(xref(0, split, FORWARD, upper, cols=cols), xref(0, split, FAR, upper, cols=cols), axis, 3)
        passed[name, split] = (one, two)
        crossed[name, split] = [
            send(xref(0, split, c, cols=cols), xref(1, split, c, cols=cols), "core") for c in (BACK, FORWARD)]

    def cross_far(name, split):
        cols = CHUNKS[name][2]
        for copy in passed[name, split]:
            copy.wait_recv()
        crossed[name, split].append(send(xref(0, split, FAR, cols=cols), xref(1, split, FAR, cols=cols), "core"))

    near = []
    for split in range(3):
        for copy in second[split]:
            copy.wait_recv()
        spread("A", split)
    for split in range(3):
        spread("B", split)
    for split in range(3):
        near.append(send(xref(0, split, 0), xref(1, split, 0), "core"))
    for split in range(3):
        spread("C", split)

    def relayout(name):
        first_tile, count, (at, width) = CHUNKS[name]
        for half in range(2):
            for split in range(3):
                span = tiles_of(name, split)
                if span is None:
                    continue

                def rows(z, _, half=half, split=split, span=span):
                    v = xs[half, split, z, :, :, :, at:at + width].astype(F32).reshape(16, 2, 8, width)
                    for h in range(2):
                        col = ((half * 2 + h) * count + span[0] - first_tile) * LANE
                        lhs[name][pl.ds(z * 128, 128), col:col + width] = v[:, h].reshape(128, width).astype(BF16)
                    return 0

                lax.fori_loop(0, 4, rows, 0)

    def multiply(name, start):
        for copy in fetches[name]:
            copy.wait()

        def one(i, _):
            product = jnp.dot(lhs[name][...], wgu[name][i], preferred_element_type=F32)
            if start:
                acc[i] = product
            else:
                acc[i] += product
            return 0

        lax.fori_loop(0, 4, one, 0)

    def arrive(name):
        for split in range(3):
            for copy in crossed[name, split]:
                copy.wait_recv()

    for split in range(3):
        pass_on("A", split)
    for split in range(3):
        pass_on("B", split)
    for split in range(3):
        cross_far("A", split)
    for copy in near:
        copy.wait_recv()
    arrive("A")
    relayout("A")
    multiply("A", True)
    for split in range(3):
        pass_on("C", split)
    for split in range(3):
        cross_far("B", split)
    arrive("B")
    relayout("B")
    multiply("B", False)
    for split in range(3):
        cross_far("C", split)
    arrive("C")
    relayout("C")
    multiply("C", False)

    lane = lax.broadcasted_iota(jnp.int32, (128, LANE), 1)

    def weigh(z, _):
        v = xs[0, 2, z, :, :, :, 512:640].astype(F32).reshape(16, 2, 8, LANE)[:, 0].reshape(128, LANE)
        for e in range(2):
            w = jnp.sum(jnp.where(lane % 32 == node * 2 + e, v, 0.0), axis=1, keepdims=True)
            scale[e, pl.ds(z * 128, 128), :] = jnp.broadcast_to(w, (128, 256))
        return 0

    lax.fori_loop(0, 4, weigh, 0)

    def activate(i, _):
        rows = pl.ds(i * 128, 128)
        for e in range(2):
            gate = acc[e, rows, :]
            hid[e, rows, :] = (gate / (1.0 + jnp.exp(-gate)) * acc[2 + e, rows, :]).astype(BF16)
        return 0

    lax.fori_loop(0, 4, activate, 0)

    for copy in fetches["D"]:
        copy.wait()

    def project(name, half, target):
        first_tile, count, (at, width) = CHUNKS[name]
        for pair in range(count // 2):
            lo = (first_tile + 2 * pair) * LANE

            def rows(m, _, lo=lo, pair=pair):
                part = pl.ds(m * 256, 256)
                parts = []
                for h in range(2):
                    cols = slice(h * QUARTER + lo, h * QUARTER + lo + 256)
                    y = scale[0, part, :] * jnp.dot(hid[0, part, :], wd[half, 0, :, cols], preferred_element_type=F32)
                    y = y + scale[1, part, :] * jnp.dot(hid[1, part, :], wd[half, 1, :, cols], preferred_element_type=F32)
                    parts.append(y.reshape(32, 8, 256))
                block = jnp.concatenate(parts, axis=1).astype(BF16).reshape(2, 4, 4, 16, 256)
                if name == "C":
                    target[0, pl.ds(m * 2, 2), :, :, :, at:at + width] = block[..., :LANE]
                    target[1, pl.ds(m * 2, 2), :, :, :, at:at + width] = block[..., LANE:]
                else:
                    target[pair, pl.ds(m * 2, 2), :, :, :, at:at + width] = block
                return 0

            lax.fori_loop(0, 2, rows, 0)

    def splits_of(name):
        return (0, 1) if name == "C" else (0, 1, 2)

    def ref_of(array, name, index):
        return array.at[index + (slice(None), pl.ds(*CHUNKS[name][2]))]

    swaps, early, late, rowed, single = {}, {}, {}, {}, {}

    def produce(name):
        project(name, 1, other_sum)
        swaps[name] = [
            send(ref_of(other_sum, name, (split,) + place(split)), ref_of(core_got, name, (split,) + place(split)), "core")
            for split in splits_of(name)]
        project(name, 0, own_sum)

    lower, upper = slice(0, 2), slice(2, 4)

    def add(name, target, extras):
        cols = pl.ds(*CHUNKS[name][2])
        total = target[0][target[1] + (slice(None), cols)].astype(F32)
        for array, index in extras:
            total = total + array[index + (slice(None), cols)].astype(F32)
        target[0][target[1] + (slice(None), cols)] = total.astype(BF16)

    def reduce_cores(name):
        cols = pl.ds(*CHUNKS[name][2])
        for copy, split in zip(swaps[name], splits_of(name)):
            copy.wait_recv()

            def slab(z, _, split=split):
                add(name, (own_sum, (split, z, slice(None), slice(None))), [(core_got, (split, z, slice(None), slice(None)))])
                return 0

            lax.fori_loop(0, 4, slab, 0)
            axis = ORDERS[split][2]
            to_forward = send(ref_of(own_sum, name, (split,) + place(split, FAR, lower)),
                              ref_of(r1, name, (split,) + plane(split, lower)), axis, 1)
            to_back = send(ref_of(own_sum, name, (split,) + place(split, FAR, upper)),
                           ref_of(r1, name, (split,) + plane(split, upper)), axis, 3)
            half_one = send(ref_of(own_sum, name, (split,) + place(split, FORWARD, upper)),
                            ref_of(r2, name, (split, 0) + plane(split, upper)), axis, 1)
            half_two = send(ref_of(own_sum, name, (split,) + place(split, BACK, lower)),
                            ref_of(r2, name, (split, 1) + plane(split, lower)), axis, 3)
            early[name, split] = (to_forward, to_back, half_one, half_two)

    def reduce_far(name):
        for split in splits_of(name):
            axis = ORDERS[split][2]
            to_forward, to_back, _, _ = early[name, split]
            to_forward.wait_recv()
            add(name, (own_sum, (split,) + place(split, FORWARD, lower)), [(r1, (split,) + plane(split, lower))])
            one = send(ref_of(own_sum, name, (split,) + place(split, FORWARD, lower)),
                       ref_of(r2, name, (split, 0) + plane(split, lower)), axis, 1)
            to_back.wait_recv()
            add(name, (own_sum, (split,) + place(split, BACK, upper)), [(r1, (split,) + plane(split, upper))])
            two = send(ref_of(own_sum, name, (split,) + place(split, BACK, upper)),
                       ref_of(r2, name, (split, 1) + plane(split, upper)), axis, 3)
            late[name, split] = (one, two)

    def reduce_plane(name):
        for split in splits_of(name):
            for copy in early[name, split][2:] + late[name, split]:
                copy.wait_recv()
            add(name, (own_sum, (split,) + place(split, 0)),
                [(r2, (split, 0) + plane(split)), (r2, (split, 1) + plane(split))])
            rowed[name, split] = [
                send(ref_of(own_sum, name, (split,) + place(split, 0, step)), ref_of(r3, name, (split, step, slice(None))), ORDERS[split][1], step)
                for step in (1, 3, 2)]

    def reduce_row(name):
        for split in splits_of(name):
            for copy in rowed[name, split]:
                copy.wait_recv()
            add(name, (own_sum, (split,) + place(split, 0, 0)), [(r3, (split, step, slice(None))) for step in (1, 2, 3)])
            single[name, split] = [
                send(ref_of(own_sum, name, (split,) + place(split, 0, 0, step)), ref_of(r4, name, (split, step)), ORDERS[split][0], step)
                for step in (1, 3, 2)]

    def reduce_last(name):
        cols = pl.ds(*CHUNKS[name][2])
        for split in splits_of(name):
            for copy in single[name, split]:
                copy.wait_recv()
            total = own_sum[split, 0, 0, 0, :, cols].astype(F32)
            for step in (1, 2, 3):
                total = total + r4[split, step, :, cols].astype(F32)
            fin[split, :, cols] = total.astype(BF16)

    produce("C")
    reduce_cores("C")
    produce("A")
    reduce_cores("A")
    reduce_far("C")
    produce("B")
    reduce_cores("B")
    reduce_far("A")
    reduce_plane("C")
    reduce_far("B")
    reduce_plane("A")
    reduce_row("C")
    reduce_plane("B")
    reduce_row("A")
    reduce_last("C")
    reduce_row("B")
    reduce_last("A")
    reduce_last("B")

    back = send(fin, fin_got, "core")
    back.wait_recv()
    for split in range(3):
        for name, (_, _, (at, width)) in CHUNKS.items():
            span = tiles_of(name, split)
            if span is None:
                continue
            a = fin[split, :, at:at + width].astype(F32)
            b = fin_got[split, :, at:at + width].astype(F32)
            for half in range(2):
                v = jnp.where(core == half, a, b)
                for h in range(2):
                    col = half * HALF + h * QUARTER + span[0] * LANE
                    rows = jnp.where(core == 0, v[8 * h:8 * h + 4], v[8 * h + 4:8 * h + 8])
                    out[:, col:col + width] = rows.astype(BF16)
    for copy in pending:
        copy.wait_send()


def on_device(tokens, expert_ids, route_weights, w_gate, w_up, w_down):
    vmem = pl.BlockSpec(memory_space=pltpu.VMEM)
    anywhere = pl.BlockSpec(memory_space=pl.ANY)
    grid3 = (3, 4, 4, 4, 16, WIDE)
    return pl.pallas_call(
        kernel,
        out_shape=jax.ShapeDtypeStruct((4, 7168), BF16),
        in_specs=[vmem, vmem, vmem, anywhere, anywhere, anywhere],
        out_specs=vmem,
        scratch_shapes=[
            pltpu.VMEM((8, HALF + LANE), F32),
            pltpu.VMEM((8, HALF + LANE), F32),
            pltpu.VMEM((8, HALF + LANE), F32),
            pltpu.VMEM((2,) + grid3, BF16),
            pltpu.VMEM((TOKENS, 24 * LANE), BF16),
            pltpu.VMEM((TOKENS, 24 * LANE), BF16),
            pltpu.VMEM((TOKENS, 8 * LANE), BF16),
            pltpu.VMEM((4, 24 * LANE, 256), BF16),
            pltpu.VMEM((4, 24 * LANE, 256), BF16),
            pltpu.VMEM((4, 8 * LANE, 256), BF16),
            pltpu.VMEM((2, 2, 256, HALF), BF16),
            pltpu.VMEM((4, TOKENS, 256), F32),
            pltpu.VMEM((2, TOKENS, 256), BF16),
            pltpu.VMEM((2, TOKENS, 256), F32),
            pltpu.VMEM(grid3, BF16),
            pltpu.VMEM(grid3, BF16),
            pltpu.VMEM(grid3, BF16),
            pltpu.VMEM((3, 4, 4, 16, WIDE), BF16),
            pltpu.VMEM((3, 2, 4, 4, 16, WIDE), BF16),
            pltpu.VMEM((3, 4, 4, 16, WIDE), BF16),
            pltpu.VMEM((3, 4, 16, WIDE), BF16),
            pltpu.VMEM((3, 16, WIDE), BF16),
            pltpu.VMEM((3, 16, WIDE), BF16),
            pltpu.SemaphoreType.DMA((N_SEMS,)),
            pltpu.SemaphoreType.DMA((N_SEMS,)),
            pltpu.SemaphoreType.DMA((32,)),
        ],
        compiler_params=pltpu.CompilerParams(
            collective_id=0, has_side_effects=True, vmem_limit_bytes=62 * 2**20),
        cost_estimate=pl.CostEstimate(flops=11_300_000_000, bytes_accessed=22_100_000, transcendentals=262_144),
    )(tokens, expert_ids, route_weights, w_gate, w_up, w_down)


def solution(mesh):
    placed = (
        P(("node", "local"), None),
        P(("node", "local"), None),
        P(("node", "local"), None),
        P("node", None, "local"),
        P("node", None, "local"),
        P("node", "local", None),
    )
    return jax.shard_map(
        on_device, mesh=mesh, in_specs=placed, out_specs=P(("node", "local"), None), check_vma=False
    )
```

```python
import jax
import jax.numpy as jnp
from jax import lax
from jax.experimental import pallas as pl
from jax.experimental.pallas import tpu as pltpu
from jax.sharding import PartitionSpec as P

MESH = pl.DeviceIdType.MESH
F32, BF16 = jnp.float32, jnp.bfloat16
LANE = 128
HALF = 3584
QUARTER = 1792
TOKENS = 512
WIDE = 640
ORDERS = ("xyz", "yzx", "zxy")
PLACE = {"z": 0, "y": 1, "x": 2}
FORWARD, BACK, FAR = 1, 3, 2
CHUNKS = {"A": (0, 6, (0, 256)), "B": (6, 6, (256, 256)), "C": (12, 2, (512, 128))}
N_SEND, N_RECV = 24, 80


def coordinates():
    node, local = lax.axis_index("node"), lax.axis_index("local")
    return {"x": local // 2, "y": node // 4, "z": node % 4, "core": local % 2}


def neighbour(axis, step):
    at = coordinates()
    if axis == "core":
        at["core"] = 1 - at["core"]
    else:
        at[axis] = lax.rem(at[axis] + step, 4)
    return (at["y"] * 4 + at["z"], at["x"] * 2 + at["core"])


def place(split, c=slice(None), b=slice(None), a=slice(None)):
    order = ORDERS[split]
    index = [None, None, None]
    for axis, value in zip(order, (a, b, c)):
        index[PLACE[axis]] = value
    return tuple(index)


def plane(split, b=slice(None), a=slice(None)):
    order = ORDERS[split]
    return tuple(v for _, v in sorted([(PLACE[order[0]], a), (PLACE[order[1]], b)], key=lambda p: p[0]))


def tiles_of(chunk, split):
    first, count, _ = CHUNKS[chunk]
    if chunk == "C":
        return (first + split, 1) if split < 2 else None
    return (first + 2 * split, 2)


def kernel(tokens, ids, weights, w_gate, w_up, w_down, out,
           own, sent, got, xs, lhs_a, lhs_b, lhs_c, wgu_a, wgu_b, wgu_c, wd, acc, hid, scale,
           own_sum, other_sum, core_got, r1, r2, r3, r4, fin, fin_got, send_sem, recv_sem, local_sem):
    core = lax.axis_index("local") % 2
    node = lax.axis_index("node")
    send_slots, recv_slots, send_totals = {}, {}, {}

    def slot(table, key):
        return table.setdefault(key, len(table))

    def send(src, dst, axis, step, recv_key, send_key):
        copy = pltpu.make_async_remote_copy(
            src_ref=src, dst_ref=dst, send_sem=send_sem.at[slot(send_slots, send_key)],
            recv_sem=recv_sem.at[slot(recv_slots, recv_key)],
            device_id=neighbour(axis, step), device_id_type=MESH)
        copy.start()

    def received(key, ref):
        pltpu.make_async_copy(ref, ref, recv_sem.at[recv_slots[key]]).wait()

    def all_sent(key, ref):
        pltpu.make_async_copy(ref, ref, send_sem.at[send_slots[key]]).wait()

    barrier = pltpu.get_barrier_semaphore()
    friends = [(axis, step) for axis in "xyz" for step in (1, 2, 3)] + [("core", 0)]
    for axis, step in friends:
        pl.semaphore_signal(barrier, inc=1, device_id=neighbour(axis, step), device_id_type=MESH)

    def fetch(src, dst, i):
        pltpu.make_async_copy(src, dst, local_sem.at[i]).start()

    def fetched(ref, i):
        pltpu.make_async_copy(ref, ref, local_sem.at[i]).wait()

    wgu = {"A": wgu_a, "B": wgu_b, "C": wgu_c}
    lhs = {"A": lhs_a, "B": lhs_b, "C": lhs_c}

    def fetch_chunk(name):
        first, count, _ = CHUNKS[name]
        for which, source in enumerate((w_gate, w_up)):
            for half in range(2):
                side = lax.rem(core + half, 2)
                for h in range(2):
                    start = pl.multiple_of(side * HALF + h * QUARTER + first * LANE, LANE)
                    fetch(source.at[:, pl.ds(start, count * LANE), :],
                          wgu[name].at[2 * which:2 * which + 2, pl.ds((half * 2 + h) * count * LANE, count * LANE), :], "ABC".index(name))

    fetch_chunk("A")

    row4 = lax.broadcasted_iota(jnp.int32, (4, LANE), 1)
    dense = jnp.zeros((4, LANE), F32)
    for k in range(8):
        dense = dense + jnp.where(row4 % 32 == ids[:, k:k + 1], weights[:, k:k + 1], 0.0)
    high = dense.astype(BF16).astype(F32)
    mid = (dense - high).astype(BF16).astype(F32)
    low = dense - high - mid
    meta = jnp.where(row4 < 32, high, jnp.where(row4 < 64, mid, jnp.where(row4 < 96, low, 0.0)))
    left = tokens[:, :HALF].astype(F32)
    right = tokens[:, HALF:].astype(F32)
    mine = jnp.where(core == 0, left, right)
    theirs = jnp.where(core == 0, right, left)
    for r in (0, 4):
        own[r:r + 4, :HALF] = mine
        own[r:r + 4, HALF:] = meta
        sent[r:r + 4, :HALF] = theirs
        sent[r:r + 4, HALF:] = meta

    pl.semaphore_wait(barrier, len(friends))

    send(sent, got, "core", 0, "entry", "entry")
    fetch_chunk("B")
    received("entry", got)
    block = jnp.where(lax.broadcasted_iota(jnp.int32, (8, HALF + LANE), 0) // 4 == core, own[...], got[...])
    for split in range(3):
        for name, (_, _, (at, width)) in CHUNKS.items():
            span = tiles_of(name, split)
            if span is None:
                piece = jnp.concatenate([block[:, HALF:], block[:, HALF:]], axis=0)
            else:
                lo = span[0] * LANE
                piece = jnp.concatenate([block[:, lo:lo + width], block[:, QUARTER + lo:QUARTER + lo + width]], axis=0)
            xs[0, split, 0, 0, 0, :, at:at + width] = piece.astype(BF16)

    def xref(half, split, c, b=slice(None), a=slice(None), cols=None):
        index = (half, split) + place(split, c, b, a)
        if cols is not None:
            index = index + (slice(None), pl.ds(*cols))
        return xs.at[index]

    for split in range(3):
        for step in (1, 3, 2):
            send(xref(0, split, 0, 0, 0), xref(0, split, 0, 0, (4 - step) % 4), ORDERS[split][0], step, ("first", split), "first")
    fetch_chunk("C")
    for half in range(2):
        side = lax.rem(core + half, 2)
        fetch(w_down.at[:, :, pl.ds(pl.multiple_of(side * HALF, LANE), HALF)], wd.at[half], 3)
    parts = ((0, 256), (256, 384))
    for split in range(3):
        received(("first", split), xref(0, split, 0, 0, slice(1, 4)))
        for part, cols in enumerate(parts):
            for step in (1, 3, 2):
                send(xref(0, split, 0, 0, cols=cols), xref(0, split, 0, (4 - step) % 4, cols=cols), ORDERS[split][1], step,
                     ("second", part, split), ("second", part))

    lower, upper = slice(0, 2), slice(2, 4)

    def spread(name, split):
        cols = CHUNKS[name][2]
        axis = ORDERS[split][2]
        send(xref(0, split, 0, cols=cols), xref(0, split, BACK, cols=cols), axis, 1, ("third", BACK, name, split), "third")
        send(xref(0, split, 0, cols=cols), xref(0, split, FORWARD, cols=cols), axis, 3, ("third", FORWARD, name, split), "third")

    def pass_on(name):
        cols = CHUNKS[name][2]
        for split in range(3):
            axis = ORDERS[split][2]
            for side, part, step in ((BACK, lower, 1), (FORWARD, upper, 3)):
                received(("third", side, name, split), xref(0, split, side, cols=cols))
                send(xref(0, split, side, part, cols=cols), xref(0, split, FAR, part, cols=cols), axis, step,
                     ("passed", name, split), "passed")
                send(xref(0, split, side, cols=cols), xref(1, split, side, cols=cols), "core", 0, ("cross", name), "cross")

    def cross_far(name):
        cols = CHUNKS[name][2]
        for split in range(3):
            received(("passed", name, split), xref(0, split, FAR, cols=cols))
            send(xref(0, split, FAR, cols=cols), xref(1, split, FAR, cols=cols), "core", 0, ("cross", name), "cross")

    def arrive(name):
        received(("cross", name), xs.at[1, :, 1:4, :, :, :, pl.ds(*CHUNKS[name][2])])

    for part, names in ((0, "A"), (1, "BC")):
        for split in range(3):
            received(("second", part, split), xref(0, split, 0, slice(1, 4), cols=parts[part]))
            for name in names:
                spread(name, split)
    for split in range(3):
        send(xref(0, split, 0), xref(1, split, 0), "core", 0, "near", "near")

    def relayout(name):
        first_tile, count, (at, width) = CHUNKS[name]
        for half in range(2):
            for split in range(3):
                span = tiles_of(name, split)
                if span is None:
                    continue

                def rows(z, _, half=half, split=split, span=span):
                    v = xs[half, split, z, :, :, :, at:at + width].astype(F32).reshape(16, 2, 8, width)
                    for h in range(2):
                        col = ((half * 2 + h) * count + span[0] - first_tile) * LANE
                        lhs[name][pl.ds(z * 128, 128), col:col + width] = v[:, h].reshape(128, width).astype(BF16)
                    return 0

                lax.fori_loop(0, 4, rows, 0)

    def multiply(name, begin, end):
        if begin == 0:
            fetched(wgu[name], "ABC".index(name))

        def one(i, _):
            product = jnp.dot(lhs[name][...], wgu[name][i], preferred_element_type=F32)
            if name == "A":
                acc[i] = product
            else:
                acc[i] += product
            return 0

        lax.fori_loop(begin, end, one, 0)

    pass_on("A")
    pass_on("B")
    cross_far("A")
    received("near", xs.at[1, :, 0])
    arrive("A")
    relayout("A")
    multiply("A", 0, 1)
    pass_on("C")
    multiply("A", 1, 2)
    cross_far("B")
    multiply("A", 2, 4)
    cross_far("C")
    arrive("B")
    relayout("B")
    multiply("B", 0, 4)
    arrive("C")
    relayout("C")
    multiply("C", 0, 4)

    lane = lax.broadcasted_iota(jnp.int32, (128, LANE), 1)

    def weigh(z, _):
        v = xs[0, 2, z, :, :, :, 512:640].astype(F32).reshape(16, 2, 8, LANE)[:, 0].reshape(128, LANE)
        for e in range(2):
            w = jnp.sum(jnp.where(lane % 32 == node * 2 + e, v, 0.0), axis=1, keepdims=True)
            scale[e, pl.ds(z * 128, 128), :] = jnp.broadcast_to(w, (128, 256))
        return 0

    lax.fori_loop(0, 4, weigh, 0)

    def activate(i, _):
        rows = pl.ds(i * 128, 128)
        for e in range(2):
            gate = acc[e, rows, :]
            hid[e, rows, :] = (gate / (1.0 + jnp.exp(-gate)) * acc[2 + e, rows, :]).astype(BF16)
        return 0

    lax.fori_loop(0, 4, activate, 0)

    fetched(wd, 3)

    def project(name, half, target):
        first_tile, count, (at, width) = CHUNKS[name]
        for pair in range(count // 2):
            lo = (first_tile + 2 * pair) * LANE

            halves = []
            for h in range(2):
                cols = slice(h * QUARTER + lo, h * QUARTER + lo + 256)
                y = scale[0] * jnp.dot(hid[0], wd[half, 0, :, cols], preferred_element_type=F32)
                y = y + scale[1] * jnp.dot(hid[1], wd[half, 1, :, cols], preferred_element_type=F32)
                halves.append(y.reshape(64, 8, 256))
            block = jnp.concatenate(halves, axis=1).astype(BF16).reshape(4, 4, 4, 16, 256)
            if name == "C":
                target[0, :, :, :, :, at:at + width] = block[..., :LANE]
                target[1, :, :, :, :, at:at + width] = block[..., LANE:]
            else:
                target[pair, :, :, :, :, at:at + width] = block

    def splits_of(name):
        return (0, 1) if name == "C" else (0, 1, 2)

    def ref_of(array, name, index):
        return array.at[index + (slice(None), pl.ds(*CHUNKS[name][2]))]

    def produce_other(name):
        project(name, 1, other_sum)
        for split in splits_of(name):
            send(ref_of(other_sum, name, (split,) + place(split)), ref_of(core_got, name, (split,) + place(split)), "core", 0,
                 ("swap", name), ("swap", name))

    def produce_own(name):
        project(name, 0, own_sum)

    def group(array, name, index=()):
        some = slice(0, len(splits_of(name)))
        return array.at[(some,) + index + (slice(None),) * (len(array.shape) - len(index) - 2) + (pl.ds(*CHUNKS[name][2]),)]

    def add(name, target, extras):
        cols = pl.ds(*CHUNKS[name][2])
        total = target[0][target[1] + (slice(None), cols)].astype(F32)
        for array, index in extras:
            total = total + array[index + (slice(None), cols)].astype(F32)
        target[0][target[1] + (slice(None), cols)] = total.astype(BF16)

    def reduce_cores(name):
        received(("swap", name), group(core_got, name))
        for split in splits_of(name):

            def slab(z, _, split=split):
                add(name, (own_sum, (split, z, slice(None), slice(None))), [(core_got, (split, z, slice(None), slice(None)))])
                return 0

            lax.fori_loop(0, 4, slab, 0)
            axis = ORDERS[split][2]
            for part, step in ((lower, 1), (upper, 3)):
                send(ref_of(own_sum, name, (split,) + place(split, FAR, part)), ref_of(r1, name, (split,) + plane(split, part)),
                     axis, step, ("far", step, name, split), ("far", name))
            for side, part, step, way in ((FORWARD, upper, 1, 0), (BACK, lower, 3, 1)):
                send(ref_of(own_sum, name, (split,) + place(split, side, part)),
                     ref_of(r2, name, (split, way) + plane(split, part)), axis, step, ("sides", name, split), ("sides", name))

    def reduce_far(name):
        for split in splits_of(name):
            axis = ORDERS[split][2]
            for side, part, step, way in ((FORWARD, lower, 1, 0), (BACK, upper, 3, 1)):
                received(("far", step, name, split), ref_of(r1, name, (split,) + plane(split, part)))
                add(name, (own_sum, (split,) + place(split, side, part)), [(r1, (split,) + plane(split, part))])
                send(ref_of(own_sum, name, (split,) + place(split, side, part)),
                     ref_of(r2, name, (split, way) + plane(split, part)), axis, step, ("sides", name, split), ("sides", name))

    def reduce_plane(name):
        for split in splits_of(name):
            received(("sides", name, split), ref_of(r2, name, (split,) + (slice(None),) * 3))
            add(name, (own_sum, (split,) + place(split, 0)),
                [(r2, (split, 0) + plane(split)), (r2, (split, 1) + plane(split))])
            for step in (1, 3, 2):
                send(ref_of(own_sum, name, (split,) + place(split, 0, step)), ref_of(r3, name, (split, step, slice(None))),
                     ORDERS[split][1], step, ("row", name, split), ("row", name))

    def reduce_row(name):
        for split in splits_of(name):
            received(("row", name, split), ref_of(r3, name, (split, slice(1, 4), slice(None))))
            add(name, (own_sum, (split,) + place(split, 0, 0)), [(r3, (split, step, slice(None))) for step in (1, 2, 3)])
            for step in (1, 3, 2):
                send(ref_of(own_sum, name, (split,) + place(split, 0, 0, step)), ref_of(r4, name, (split, step)),
                     ORDERS[split][0], step, ("one", name), ("one", name))

    def reduce_last(name):
        cols = pl.ds(*CHUNKS[name][2])
        received(("one", name), group(r4, name, (slice(1, 4),)))
        for split in splits_of(name):
            total = own_sum[split, 0, 0, 0, :, cols].astype(F32)
            for step in (1, 2, 3):
                total = total + r4[split, step, :, cols].astype(F32)
            fin[split, :, cols] = total.astype(BF16)

    produce_other("C")
    produce_own("C")
    produce_other("A")
    reduce_cores("C")
    produce_own("A")
    reduce_cores("A")
    produce_other("B")
    reduce_far("C")
    produce_own("B")
    reduce_cores("B")
    reduce_plane("C")
    reduce_far("A")
    reduce_row("C")
    reduce_far("B")
    reduce_plane("A")
    reduce_last("C")
    reduce_plane("B")
    reduce_row("A")
    reduce_row("B")
    reduce_last("A")
    reduce_last("B")

    send(fin, fin_got, "core", 0, "last", "last")
    received("last", fin_got)
    for split in range(3):
        for name, (_, _, (at, width)) in CHUNKS.items():
            span = tiles_of(name, split)
            if span is None:
                continue
            a = fin[split, :, at:at + width].astype(F32)
            b = fin_got[split, :, at:at + width].astype(F32)
            for half in range(2):
                v = jnp.where(core == half, a, b)
                for h in range(2):
                    col = half * HALF + h * QUARTER + span[0] * LANE
                    rows = jnp.where(core == 0, v[8 * h:8 * h + 4], v[8 * h + 4:8 * h + 8])
                    out[:, col:col + width] = rows.astype(BF16)
    all_sent("entry", got)
    all_sent("first", xs.at[0, :, 0, 0, 1:4])
    for part, cols in enumerate(parts):
        all_sent(("second", part), xs.at[0, :, 0, 1:4, :, :, pl.ds(*cols)])
    all_sent("third", xs.at[0, :, 1:3])
    all_sent("passed", xs.at[0, :, 1])
    all_sent("near", xs.at[1, :, 0])
    all_sent("cross", xs.at[1, :, 1:4])
    for name in CHUNKS:
        all_sent(("swap", name), group(core_got, name))
        all_sent(("far", name), group(r1, name))
        all_sent(("sides", name), group(r2, name))
        all_sent(("row", name), group(r3, name, (slice(1, 4),)))
        all_sent(("one", name), group(r4, name, (slice(1, 4),)))
    all_sent("last", fin_got)


def on_device(tokens, expert_ids, route_weights, w_gate, w_up, w_down):
    vmem = pl.BlockSpec(memory_space=pltpu.VMEM)
    anywhere = pl.BlockSpec(memory_space=pl.ANY)
    grid3 = (3, 4, 4, 4, 16, WIDE)
    return pl.pallas_call(
        kernel,
        out_shape=jax.ShapeDtypeStruct((4, 7168), BF16),
        in_specs=[vmem, vmem, vmem, anywhere, anywhere, anywhere],
        out_specs=vmem,
        scratch_shapes=[
            pltpu.VMEM((8, HALF + LANE), F32),
            pltpu.VMEM((8, HALF + LANE), F32),
            pltpu.VMEM((8, HALF + LANE), F32),
            pltpu.VMEM((2,) + grid3, BF16),
            pltpu.VMEM((TOKENS, 24 * LANE), BF16),
            pltpu.VMEM((TOKENS, 24 * LANE), BF16),
            pltpu.VMEM((TOKENS, 8 * LANE), BF16),
            pltpu.VMEM((4, 24 * LANE, 256), BF16),
            pltpu.VMEM((4, 24 * LANE, 256), BF16),
            pltpu.VMEM((4, 8 * LANE, 256), BF16),
            pltpu.VMEM((2, 2, 256, HALF), BF16),
            pltpu.VMEM((4, TOKENS, 256), F32),
            pltpu.VMEM((2, TOKENS, 256), BF16),
            pltpu.VMEM((2, TOKENS, 256), F32),
            pltpu.VMEM(grid3, BF16),
            pltpu.VMEM(grid3, BF16),
            pltpu.VMEM(grid3, BF16),
            pltpu.VMEM((3, 4, 4, 16, WIDE), BF16),
            pltpu.VMEM((3, 2, 4, 4, 16, WIDE), BF16),
            pltpu.VMEM((3, 4, 4, 16, WIDE), BF16),
            pltpu.VMEM((3, 4, 16, WIDE), BF16),
            pltpu.VMEM((3, 16, WIDE), BF16),
            pltpu.VMEM((3, 16, WIDE), BF16),
            pltpu.SemaphoreType.DMA((N_SEND,)),
            pltpu.SemaphoreType.DMA((N_RECV,)),
            pltpu.SemaphoreType.DMA((4,)),
        ],
        compiler_params=pltpu.CompilerParams(
            collective_id=0, has_side_effects=True, vmem_limit_bytes=62 * 2**20),
        cost_estimate=pl.CostEstimate(flops=11_300_000_000, bytes_accessed=22_100_000, transcendentals=262_144),
    )(tokens, expert_ids, route_weights, w_gate, w_up, w_down)


def solution(mesh):
    placed = (
        P(("node", "local"), None),
        P(("node", "local"), None),
        P(("node", "local"), None),
        P("node", None, "local"),
        P("node", None, "local"),
        P("node", "local", None),
    )
    return jax.shard_map(
        on_device, mesh=mesh, in_specs=placed, out_specs=P(("node", "local"), None), check_vma=False
    )
```

```python
import jax
import jax.numpy as jnp
from jax import lax
from jax.experimental import pallas as pl
from jax.experimental.pallas import tpu as pltpu
from jax.sharding import PartitionSpec as P

MESH = pl.DeviceIdType.MESH
F32, BF16 = jnp.float32, jnp.bfloat16
LANE = 128
HALF = 3584
QUARTER = 1792
TOKENS = 512
WIDE = 640
ORDERS = ("xyz", "yzx", "zxy")
PLACE = {"z": 0, "y": 1, "x": 2}
FORWARD, BACK, FAR = 1, 3, 2
CHUNKS = {"A": (0, 6, (0, 256)), "B": (6, 6, (256, 256)), "C": (12, 2, (512, 128))}
N_SEND, N_RECV = 22, 85


def coordinates():
    node, local = lax.axis_index("node"), lax.axis_index("local")
    return {"x": local // 2, "y": node // 4, "z": node % 4, "core": local % 2}


def neighbour(axis, step):
    at = coordinates()
    if axis == "core":
        at["core"] = 1 - at["core"]
    else:
        at[axis] = lax.rem(at[axis] + step, 4)
    return (at["y"] * 4 + at["z"], at["x"] * 2 + at["core"])


def place(split, c=slice(None), b=slice(None), a=slice(None)):
    order = ORDERS[split]
    index = [None, None, None]
    for axis, value in zip(order, (a, b, c)):
        index[PLACE[axis]] = value
    return tuple(index)


def plane(split, b=slice(None), a=slice(None)):
    order = ORDERS[split]
    return tuple(v for _, v in sorted([(PLACE[order[0]], a), (PLACE[order[1]], b)], key=lambda p: p[0]))


def tiles_of(chunk, split):
    first, count, _ = CHUNKS[chunk]
    if chunk == "C":
        return (first + split, 1) if split < 2 else None
    return (first + 2 * split, 2)


def kernel(tokens, ids, weights, w_gate, w_up, w_down, out,
           own, sent, got, xs, lhs_a, lhs_b, lhs_c, wgu_a, wgu_b, wgu_c, wd, acc, hid, scale,
           own_sum, other_sum, core_got, r1, r2, r3, r4, fin, fin_got, send_sem, recv_sem, local_sem):
    core = lax.axis_index("local") % 2
    node = lax.axis_index("node")
    send_slots, recv_slots, send_totals = {}, {}, {}

    def slot(table, key):
        return table.setdefault(key, len(table))

    def send(src, dst, axis, step, recv_key, send_key):
        copy = pltpu.make_async_remote_copy(
            src_ref=src, dst_ref=dst, send_sem=send_sem.at[slot(send_slots, send_key)],
            recv_sem=recv_sem.at[slot(recv_slots, recv_key)],
            device_id=neighbour(axis, step), device_id_type=MESH)
        copy.start()

    def received(key, ref):
        pltpu.make_async_copy(ref, ref, recv_sem.at[recv_slots[key]]).wait()

    def all_sent(key, ref):
        pltpu.make_async_copy(ref, ref, send_sem.at[send_slots[key]]).wait()

    barrier = pltpu.get_barrier_semaphore()
    friends = [(axis, step) for axis in "xyz" for step in (1, 2, 3)] + [("core", 0)]
    for axis, step in friends:
        pl.semaphore_signal(barrier, inc=1, device_id=neighbour(axis, step), device_id_type=MESH)

    def fetch(src, dst, i):
        pltpu.make_async_copy(src, dst, local_sem.at[i]).start()

    def fetched(ref, i):
        pltpu.make_async_copy(ref, ref, local_sem.at[i]).wait()

    wgu = {"A": wgu_a, "B": wgu_b, "C": wgu_c}
    lhs = {"A": lhs_a, "B": lhs_b, "C": lhs_c}

    def fetch_chunk(name):
        first, count, _ = CHUNKS[name]
        for which, source in enumerate((w_gate, w_up)):
            for half in range(2):
                side = lax.rem(core + half, 2)
                for h in range(2):
                    start = pl.multiple_of(side * HALF + h * QUARTER + first * LANE, LANE)
                    fetch(source.at[:, pl.ds(start, count * LANE), :],
                          wgu[name].at[2 * which:2 * which + 2, pl.ds((half * 2 + h) * count * LANE, count * LANE), :], "ABC".index(name))

    fetch_chunk("A")

    row4 = lax.broadcasted_iota(jnp.int32, (4, LANE), 1)
    dense = jnp.zeros((4, LANE), F32)
    for k in range(8):
        dense = dense + jnp.where(row4 % 32 == ids[:, k:k + 1], weights[:, k:k + 1], 0.0)
    high = dense.astype(BF16).astype(F32)
    mid = (dense - high).astype(BF16).astype(F32)
    low = dense - high - mid
    meta = jnp.where(row4 < 32, high, jnp.where(row4 < 64, mid, jnp.where(row4 < 96, low, 0.0)))
    left = tokens[:, :HALF].astype(F32)
    right = tokens[:, HALF:].astype(F32)
    mine = jnp.where(core == 0, left, right)
    theirs = jnp.where(core == 0, right, left)
    for r in (0, 4):
        own[r:r + 4, :HALF] = mine
        own[r:r + 4, HALF:] = meta
        sent[r:r + 4, :HALF] = theirs
        sent[r:r + 4, HALF:] = meta

    pl.semaphore_wait(barrier, len(friends))

    send(sent, got, "core", 0, "entry", "entry")
    fetch_chunk("B")
    received("entry", got)
    block = jnp.where(lax.broadcasted_iota(jnp.int32, (8, HALF + LANE), 0) // 4 == core, own[...], got[...])
    for split in range(3):
        for name, (_, _, (at, width)) in CHUNKS.items():
            span = tiles_of(name, split)
            if span is None:
                piece = jnp.concatenate([block[:, HALF:], block[:, HALF:]], axis=0)
            else:
                lo = span[0] * LANE
                piece = jnp.concatenate([block[:, lo:lo + width], block[:, QUARTER + lo:QUARTER + lo + width]], axis=0)
            xs[0, split, 0, 0, 0, :, at:at + width] = piece.astype(BF16)

    def xref(half, split, c, b=slice(None), a=slice(None), cols=None):
        index = (half, split) + place(split, c, b, a)
        if cols is not None:
            index = index + (slice(None), pl.ds(*cols))
        return xs.at[index]

    for split in range(3):
        for step in (1, 3, 2):
            send(xref(0, split, 0, 0, 0), xref(0, split, 0, 0, (4 - step) % 4), ORDERS[split][0], step, ("first", split), "first")
    fetch_chunk("C")
    for half in range(2):
        side = lax.rem(core + half, 2)
        fetch(w_down.at[:, :, pl.ds(pl.multiple_of(side * HALF, LANE), HALF)], wd.at[half], 3)
    for split in range(3):
        received(("first", split), xref(0, split, 0, 0, slice(1, 4)))
        for name in "CAB":
            cols = CHUNKS[name][2]
            for step in (1, 3, 2):
                send(xref(0, split, 0, 0, cols=cols), xref(0, split, 0, (4 - step) % 4, cols=cols), ORDERS[split][1], step,
                     ("second", name, split), "second")

    lower, upper = slice(0, 2), slice(2, 4)

    def spread(name, split):
        cols = CHUNKS[name][2]
        axis = ORDERS[split][2]
        send(xref(0, split, 0, cols=cols), xref(0, split, BACK, cols=cols), axis, 1, ("third", BACK, name, split), "third")
        send(xref(0, split, 0, cols=cols), xref(0, split, FORWARD, cols=cols), axis, 3, ("third", FORWARD, name, split), "third")

    def pass_on(name):
        cols = CHUNKS[name][2]
        for split in range(3):
            axis = ORDERS[split][2]
            for side, part, step in ((BACK, lower, 1), (FORWARD, upper, 3)):
                received(("third", side, name, split), xref(0, split, side, cols=cols))
                send(xref(0, split, side, part, cols=cols), xref(0, split, FAR, part, cols=cols), axis, step,
                     ("passed", name, split), "passed")
                send(xref(0, split, side, cols=cols), xref(1, split, side, cols=cols), "core", 0, ("cross", name), "cross")

    def cross_far(name):
        cols = CHUNKS[name][2]
        for split in range(3):
            received(("passed", name, split), xref(0, split, FAR, cols=cols))
            send(xref(0, split, FAR, cols=cols), xref(1, split, FAR, cols=cols), "core", 0, ("cross", name), "cross")

    def cross_near(name):
        cols = CHUNKS[name][2]
        for split in range(3):
            send(xref(0, split, 0, cols=cols), xref(1, split, 0, cols=cols), "core", 0, ("cross", name), "cross")

    def arrive(name):
        received(("cross", name), xs.at[1, :, :, :, :, :, pl.ds(*CHUNKS[name][2])])

    def finish_second(name):
        for split in range(3):
            received(("second", name, split), xref(0, split, 0, slice(1, 4), cols=CHUNKS[name][2]))
            spread(name, split)

    def relayout(name, half):
        first_tile, count, (at, width) = CHUNKS[name]
        for split in range(3):
            span = tiles_of(name, split)
            if span is None:
                continue

            def rows(z, _, split=split, span=span):
                v = xs[half, split, z, :, :, :, at:at + width].astype(F32).reshape(16, 2, 8, width)
                for h in range(2):
                    col = ((half * 2 + h) * count + span[0] - first_tile) * LANE
                    lhs[name][pl.ds(z * 128, 128), col:col + width] = v[:, h].reshape(128, width).astype(BF16)
                return 0

            lax.fori_loop(0, 4, rows, 0)

    def multiply(name, half, begin, end):
        if half == 0 and begin == 0:
            fetched(wgu[name], "ABC".index(name))
        depth = 2 * CHUNKS[name][1] * LANE
        span = slice(half * depth, half * depth + depth)

        def one(i, _):
            product = jnp.dot(lhs[name][:, span], wgu[name][i, span], preferred_element_type=F32)
            if name == "C" and half == 0:
                acc[i] = product
            else:
                acc[i] += product
            return 0

        lax.fori_loop(begin, end, one, 0)

    finish_second("C")
    cross_near("C")
    finish_second("A")
    pass_on("C")
    finish_second("B")
    cross_near("A")
    pass_on("A")
    cross_far("C")
    relayout("C", 0)
    multiply("C", 0, 0, 4)
    arrive("C")
    relayout("C", 1)
    multiply("C", 1, 0, 4)
    pass_on("B")
    cross_far("A")
    cross_near("B")
    relayout("A", 0)
    multiply("A", 0, 0, 4)
    arrive("A")
    relayout("A", 1)
    multiply("A", 1, 0, 2)
    cross_far("B")
    multiply("A", 1, 2, 4)
    relayout("B", 0)
    multiply("B", 0, 0, 4)
    arrive("B")
    relayout("B", 1)
    multiply("B", 1, 0, 4)

    lane = lax.broadcasted_iota(jnp.int32, (128, LANE), 1)

    def weigh(z, _):
        v = xs[0, 2, z, :, :, :, 512:640].astype(F32).reshape(16, 2, 8, LANE)[:, 0].reshape(128, LANE)
        for e in range(2):
            w = jnp.sum(jnp.where(lane % 32 == node * 2 + e, v, 0.0), axis=1, keepdims=True)
            scale[e, pl.ds(z * 128, 128), :] = jnp.broadcast_to(w, (128, 256))
        return 0

    lax.fori_loop(0, 4, weigh, 0)

    def activate(i, _):
        rows = pl.ds(i * 128, 128)
        for e in range(2):
            gate = acc[e, rows, :]
            hid[e, rows, :] = (gate / (1.0 + jnp.exp(-gate)) * acc[2 + e, rows, :]).astype(BF16)
        return 0

    lax.fori_loop(0, 4, activate, 0)

    fetched(wd, 3)

    def project(name, half, target, pairs):
        first_tile, count, (at, width) = CHUNKS[name]
        for pair in pairs:
            lo = (first_tile + 2 * pair) * LANE

            halves = []
            for h in range(2):
                cols = slice(h * QUARTER + lo, h * QUARTER + lo + 256)
                y = scale[0] * jnp.dot(hid[0], wd[half, 0, :, cols], preferred_element_type=F32)
                y = y + scale[1] * jnp.dot(hid[1], wd[half, 1, :, cols], preferred_element_type=F32)
                halves.append(y.reshape(64, 8, 256))
            block = jnp.concatenate(halves, axis=1).astype(BF16).reshape(4, 4, 4, 16, 256)
            if name == "C":
                target[0, :, :, :, :, at:at + width] = block[..., :LANE]
                target[1, :, :, :, :, at:at + width] = block[..., LANE:]
            else:
                target[pair, :, :, :, :, at:at + width] = block

    def splits_of(name):
        return (0, 1) if name == "C" else (0, 1, 2)

    def ref_of(array, name, index):
        return array.at[index + (slice(None), pl.ds(*CHUNKS[name][2]))]

    def produce_other(name, pair=0):
        project(name, 1, other_sum, (pair,))
        for split in (splits_of(name) if name == "C" else (pair,)):
            send(ref_of(other_sum, name, (split,) + place(split)), ref_of(core_got, name, (split,) + place(split)), "core", 0,
                 ("swap", name, split), ("swap", name))

    def produce_own(name, pair=0):
        project(name, 0, own_sum, (pair,))

    def group(array, name, index=()):
        some = slice(0, len(splits_of(name)))
        return array.at[(some,) + index + (slice(None),) * (len(array.shape) - len(index) - 2) + (pl.ds(*CHUNKS[name][2]),)]

    def add(name, target, extras):
        cols = pl.ds(*CHUNKS[name][2])
        total = target[0][target[1] + (slice(None), cols)].astype(F32)
        for array, index in extras:
            total = total + array[index + (slice(None), cols)].astype(F32)
        target[0][target[1] + (slice(None), cols)] = total.astype(BF16)

    def reduce_cores(name, splits):
        for split in splits:
            received(("swap", name, split), ref_of(core_got, name, (split,) + place(split)))

            def slab(z, _, split=split):
                add(name, (own_sum, (split, z, slice(None), slice(None))), [(core_got, (split, z, slice(None), slice(None)))])
                return 0

            lax.fori_loop(0, 4, slab, 0)
            axis = ORDERS[split][2]
            if name == "C":
                for side, step, array, index in ((FAR, 2, r1, (split,)), (FORWARD, 1, r2, (split, 0)), (BACK, 3, r2, (split, 1))):
                    key = "far" if side == FAR else "sides"
                    send(ref_of(own_sum, name, (split,) + place(split, side)), ref_of(array, name, index + plane(split)),
                         axis, step, (key, name, split), (key, name))
                continue
            for part, step in ((lower, 1), (upper, 3)):
                send(ref_of(own_sum, name, (split,) + place(split, FAR, part)), ref_of(r1, name, (split,) + plane(split, part)),
                     axis, step, ("far", step, name, split), ("far", name))
            for side, part, step, way in ((FORWARD, upper, 1, 0), (BACK, lower, 3, 1)):
                send(ref_of(own_sum, name, (split,) + place(split, side, part)),
                     ref_of(r2, name, (split, way) + plane(split, part)), axis, step, ("sides", name, split), ("sides", name))

    def reduce_far(name):
        for split in splits_of(name):
            axis = ORDERS[split][2]
            for side, part, step, way in ((FORWARD, lower, 1, 0), (BACK, upper, 3, 1)):
                received(("far", step, name, split), ref_of(r1, name, (split,) + plane(split, part)))
                add(name, (own_sum, (split,) + place(split, side, part)), [(r1, (split,) + plane(split, part))])
                send(ref_of(own_sum, name, (split,) + place(split, side, part)),
                     ref_of(r2, name, (split, way) + plane(split, part)), axis, step, ("sides", name, split), ("sides", name))

    def reduce_plane(name):
        for split in splits_of(name):
            received(("sides", name, split), ref_of(r2, name, (split,) + (slice(None),) * 3))
            parts = [(r2, (split, 0) + plane(split)), (r2, (split, 1) + plane(split))]
            if name == "C":
                received(("far", name, split), ref_of(r1, name, (split,) + plane(split)))
                parts.append((r1, (split,) + plane(split)))
            add(name, (own_sum, (split,) + place(split, 0)), parts)
            for step in (1, 3, 2):
                send(ref_of(own_sum, name, (split,) + place(split, 0, step)), ref_of(r3, name, (split, step, slice(None))),
                     ORDERS[split][1], step, ("row", name, split), ("row", name))

    def reduce_row(name):
        for split in splits_of(name):
            received(("row", name, split), ref_of(r3, name, (split, slice(1, 4), slice(None))))
            add(name, (own_sum, (split,) + place(split, 0, 0)), [(r3, (split, step, slice(None))) for step in (1, 2, 3)])
            for step in (1, 3, 2):
                send(ref_of(own_sum, name, (split,) + place(split, 0, 0, step)), ref_of(r4, name, (split, step)),
                     ORDERS[split][0], step, ("one", name), ("one", name))

    def reduce_last(name):
        cols = pl.ds(*CHUNKS[name][2])
        received(("one", name), group(r4, name, (slice(1, 4),)))
        for split in splits_of(name):
            total = own_sum[split, 0, 0, 0, :, cols].astype(F32)
            for step in (1, 2, 3):
                total = total + r4[split, step, :, cols].astype(F32)
            fin[split, :, cols] = total.astype(BF16)

    for split in range(3):
        produce_other("A", split)
    for split in range(3):
        produce_own("A", split)
        reduce_cores("A", (split,))
    for split in range(3):
        produce_other("B", split)
    produce_other("C")
    for split in range(3):
        produce_own("B", split)
        reduce_cores("B", (split,))
    produce_own("C")
    reduce_far("A")
    reduce_cores("C", (0, 1))
    reduce_far("B")
    reduce_plane("A")
    reduce_plane("B")
    reduce_plane("C")
    reduce_row("A")
    reduce_row("B")
    reduce_row("C")
    for name in "ABC":
        reduce_last(name)

    send(fin, fin_got, "core", 0, "last", "last")
    received("last", fin_got)
    for split in range(3):
        for name, (_, _, (at, width)) in CHUNKS.items():
            span = tiles_of(name, split)
            if span is None:
                continue
            a = fin[split, :, at:at + width].astype(F32)
            b = fin_got[split, :, at:at + width].astype(F32)
            for half in range(2):
                v = jnp.where(core == half, a, b)
                for h in range(2):
                    col = half * HALF + h * QUARTER + span[0] * LANE
                    rows = jnp.where(core == 0, v[8 * h:8 * h + 4], v[8 * h + 4:8 * h + 8])
                    out[:, col:col + width] = rows.astype(BF16)
    all_sent("entry", got)
    all_sent("first", xs.at[0, :, 0, 0, 1:4])
    all_sent("second", xs.at[0, :, 0, 1:4])
    all_sent("third", xs.at[0, :, 1:3])
    all_sent("passed", xs.at[0, :, 1])
    all_sent("cross", xs.at[1])
    for name in CHUNKS:
        all_sent(("swap", name), group(core_got, name))
        all_sent(("far", name), group(r1, name))
        all_sent(("sides", name), group(r2, name))
        all_sent(("row", name), group(r3, name, (slice(1, 4),)))
        all_sent(("one", name), group(r4, name, (slice(1, 4),)))
    all_sent("last", fin_got)


def on_device(tokens, expert_ids, route_weights, w_gate, w_up, w_down):
    vmem = pl.BlockSpec(memory_space=pltpu.VMEM)
    anywhere = pl.BlockSpec(memory_space=pl.ANY)
    grid3 = (3, 4, 4, 4, 16, WIDE)
    return pl.pallas_call(
        kernel,
        out_shape=jax.ShapeDtypeStruct((4, 7168), BF16),
        in_specs=[vmem, vmem, vmem, anywhere, anywhere, anywhere],
        out_specs=vmem,
        scratch_shapes=[
            pltpu.VMEM((8, HALF + LANE), F32),
            pltpu.VMEM((8, HALF + LANE), F32),
            pltpu.VMEM((8, HALF + LANE), F32),
            pltpu.VMEM((2,) + grid3, BF16),
            pltpu.VMEM((TOKENS, 24 * LANE), BF16),
            pltpu.VMEM((TOKENS, 24 * LANE), BF16),
            pltpu.VMEM((TOKENS, 8 * LANE), BF16),
            pltpu.VMEM((4, 24 * LANE, 256), BF16),
            pltpu.VMEM((4, 24 * LANE, 256), BF16),
            pltpu.VMEM((4, 8 * LANE, 256), BF16),
            pltpu.VMEM((2, 2, 256, HALF), BF16),
            pltpu.VMEM((4, TOKENS, 256), F32),
            pltpu.VMEM((2, TOKENS, 256), BF16),
            pltpu.VMEM((2, TOKENS, 256), F32),
            pltpu.VMEM(grid3, BF16),
            pltpu.VMEM(grid3, BF16),
            pltpu.VMEM(grid3, BF16),
            pltpu.VMEM((3, 4, 4, 16, WIDE), BF16),
            pltpu.VMEM((3, 2, 4, 4, 16, WIDE), BF16),
            pltpu.VMEM((3, 4, 4, 16, WIDE), BF16),
            pltpu.VMEM((3, 4, 16, WIDE), BF16),
            pltpu.VMEM((3, 16, WIDE), BF16),
            pltpu.VMEM((3, 16, WIDE), BF16),
            pltpu.SemaphoreType.DMA((N_SEND,)),
            pltpu.SemaphoreType.DMA((N_RECV,)),
            pltpu.SemaphoreType.DMA((4,)),
        ],
        compiler_params=pltpu.CompilerParams(
            collective_id=0, has_side_effects=True, vmem_limit_bytes=62 * 2**20),
        cost_estimate=pl.CostEstimate(flops=11_300_000_000, bytes_accessed=22_100_000, transcendentals=262_144),
    )(tokens, expert_ids, route_weights, w_gate, w_up, w_down)


def solution(mesh):
    placed = (
        P(("node", "local"), None),
        P(("node", "local"), None),
        P(("node", "local"), None),
        P("node", None, "local"),
        P("node", None, "local"),
        P("node", "local", None),
    )
    return jax.shard_map(
        on_device, mesh=mesh, in_specs=placed, out_specs=P(("node", "local"), None), check_vma=False
    )
```

```python
import jax
import jax.numpy as jnp
from jax import lax
from jax.experimental import pallas as pl
from jax.experimental.pallas import tpu as pltpu
from jax.sharding import PartitionSpec as P

MESH = pl.DeviceIdType.MESH
F32, BF16 = jnp.float32, jnp.bfloat16
LANE = 128
HALF = 3584
QUARTER = 1792
TOKENS = 512
WIDE = 640
ORDERS = ("xyz", "yzx", "zxy")
PLACE = {"z": 0, "y": 1, "x": 2}
FORWARD, BACK, FAR = 1, 3, 2
CHUNKS = {"A": (0, 6, (0, 256)), "B": (6, 6, (256, 256)), "C": (12, 2, (512, 128))}
N_SEND, N_RECV = 22, 85


def coordinates():
    node, local = lax.axis_index("node"), lax.axis_index("local")
    return {"x": local // 2, "y": node // 4, "z": node % 4, "core": local % 2}


def neighbour(axis, step):
    at = coordinates()
    if axis == "core":
        at["core"] = 1 - at["core"]
    else:
        at[axis] = lax.rem(at[axis] + step, 4)
    return (at["y"] * 4 + at["z"], at["x"] * 2 + at["core"])


def place(split, c=slice(None), b=slice(None), a=slice(None)):
    order = ORDERS[split]
    index = [None, None, None]
    for axis, value in zip(order, (a, b, c)):
        index[PLACE[axis]] = value
    return tuple(index)


def plane(split, b=slice(None), a=slice(None)):
    order = ORDERS[split]
    return tuple(v for _, v in sorted([(PLACE[order[0]], a), (PLACE[order[1]], b)], key=lambda p: p[0]))


def tiles_of(chunk, split):
    first, count, _ = CHUNKS[chunk]
    if chunk == "C":
        return (first + split, 1) if split < 2 else None
    return (first + 2 * split, 2)


def kernel(tokens, ids, weights, w_gate, w_up, w_down, out,
           own, sent, got, xs, lhs_a, lhs_b, lhs_c, wgu_a, wgu_b, wgu_c, wd, acc, hid, scale,
           own_sum, other_sum, core_got, r1, r2, r3, r4, fin, fin_got, send_sem, recv_sem, local_sem):
    core = lax.axis_index("local") % 2
    node = lax.axis_index("node")
    send_slots, recv_slots, send_totals = {}, {}, {}

    def slot(table, key):
        return table.setdefault(key, len(table))

    def send(src, dst, axis, step, recv_key, send_key):
        copy = pltpu.make_async_remote_copy(
            src_ref=src, dst_ref=dst, send_sem=send_sem.at[slot(send_slots, send_key)],
            recv_sem=recv_sem.at[slot(recv_slots, recv_key)],
            device_id=neighbour(axis, step), device_id_type=MESH)
        copy.start()

    def received(key, ref):
        pltpu.make_async_copy(ref, ref, recv_sem.at[recv_slots[key]]).wait()

    def all_sent(key, ref):
        pltpu.make_async_copy(ref, ref, send_sem.at[send_slots[key]]).wait()

    barrier = pltpu.get_barrier_semaphore()
    friends = [(axis, step) for axis in "xyz" for step in (1, 2, 3)] + [("core", 0)]
    for axis, step in friends:
        pl.semaphore_signal(barrier, inc=1, device_id=neighbour(axis, step), device_id_type=MESH)

    def fetch(src, dst, i):
        pltpu.make_async_copy(src, dst, local_sem.at[i]).start()

    def fetched(ref, i):
        pltpu.make_async_copy(ref, ref, local_sem.at[i]).wait()

    wgu = {"A": wgu_a, "B": wgu_b, "C": wgu_c}
    lhs = {"A": lhs_a, "B": lhs_b, "C": lhs_c}

    def fetch_chunk(name):
        first, count, _ = CHUNKS[name]
        for which, source in enumerate((w_gate, w_up)):
            for half in range(2):
                side = lax.rem(core + half, 2)
                for h in range(2):
                    start = pl.multiple_of(side * HALF + h * QUARTER + first * LANE, LANE)
                    fetch(source.at[:, pl.ds(start, count * LANE), :],
                          wgu[name].at[:, pl.ds((half * 2 + h) * count * LANE, count * LANE), 256 * which:256 * which + 256], "ABC".index(name))

    fetch_chunk("A")

    row4 = lax.broadcasted_iota(jnp.int32, (4, LANE), 1)
    dense = jnp.zeros((4, LANE), F32)
    for k in range(8):
        dense = dense + jnp.where(row4 % 32 == ids[:, k:k + 1], weights[:, k:k + 1], 0.0)
    high = dense.astype(BF16).astype(F32)
    mid = (dense - high).astype(BF16).astype(F32)
    low = dense - high - mid
    meta = jnp.where(row4 < 32, high, jnp.where(row4 < 64, mid, jnp.where(row4 < 96, low, 0.0)))
    left = tokens[:, :HALF].astype(F32)
    right = tokens[:, HALF:].astype(F32)
    mine = jnp.where(core == 0, left, right)
    theirs = jnp.where(core == 0, right, left)
    for r in (0, 4):
        own[r:r + 4, :HALF] = mine
        own[r:r + 4, HALF:] = meta
        sent[r:r + 4, :HALF] = theirs
        sent[r:r + 4, HALF:] = meta

    pl.semaphore_wait(barrier, len(friends))

    send(sent, got, "core", 0, "entry", "entry")
    fetch_chunk("B")
    received("entry", got)
    block = jnp.where(lax.broadcasted_iota(jnp.int32, (8, HALF + LANE), 0) // 4 == core, own[...], got[...])
    for split in range(3):
        for name, (_, _, (at, width)) in CHUNKS.items():
            span = tiles_of(name, split)
            if span is None:
                piece = jnp.concatenate([block[:, HALF:], block[:, HALF:]], axis=0)
            else:
                lo = span[0] * LANE
                piece = jnp.concatenate([block[:, lo:lo + width], block[:, QUARTER + lo:QUARTER + lo + width]], axis=0)
            xs[0, split, 0, 0, 0, :, at:at + width] = piece.astype(BF16)

    def xref(half, split, c, b=slice(None), a=slice(None), cols=None):
        index = (half, split) + place(split, c, b, a)
        if cols is not None:
            index = index + (slice(None), pl.ds(*cols))
        return xs.at[index]

    for split in range(3):
        for step in (1, 3, 2):
            send(xref(0, split, 0, 0, 0), xref(0, split, 0, 0, (4 - step) % 4), ORDERS[split][0], step, ("first", split), "first")
    fetch_chunk("C")
    for half in range(2):
        side = lax.rem(core + half, 2)
        fetch(w_down.at[:, :, pl.ds(pl.multiple_of(side * HALF, LANE), HALF)], wd.at[half], 3)
    for split in range(3):
        received(("first", split), xref(0, split, 0, 0, slice(1, 4)))
        for name in "CAB":
            cols = CHUNKS[name][2]
            for step in (1, 3, 2):
                send(xref(0, split, 0, 0, cols=cols), xref(0, split, 0, (4 - step) % 4, cols=cols), ORDERS[split][1], step,
                     ("second", name, split), "second")

    lower, upper = slice(0, 2), slice(2, 4)

    def spread(name, split):
        cols = CHUNKS[name][2]
        axis = ORDERS[split][2]
        send(xref(0, split, 0, cols=cols), xref(0, split, BACK, cols=cols), axis, 1, ("third", BACK, name, split), "third")
        send(xref(0, split, 0, cols=cols), xref(0, split, FORWARD, cols=cols), axis, 3, ("third", FORWARD, name, split), "third")

    def pass_on(name):
        cols = CHUNKS[name][2]
        for split in range(3):
            axis = ORDERS[split][2]
            for side, part, step in ((BACK, lower, 1), (FORWARD, upper, 3)):
                received(("third", side, name, split), xref(0, split, side, cols=cols))
                send(xref(0, split, side, part, cols=cols), xref(0, split, FAR, part, cols=cols), axis, step,
                     ("passed", name, split), "passed")
                send(xref(0, split, side, cols=cols), xref(1, split, side, cols=cols), "core", 0, ("cross", name), "cross")

    def cross_far(name):
        cols = CHUNKS[name][2]
        for split in range(3):
            received(("passed", name, split), xref(0, split, FAR, cols=cols))
            send(xref(0, split, FAR, cols=cols), xref(1, split, FAR, cols=cols), "core", 0, ("cross", name), "cross")

    def cross_near(name):
        cols = CHUNKS[name][2]
        for split in range(3):
            send(xref(0, split, 0, cols=cols), xref(1, split, 0, cols=cols), "core", 0, ("cross", name), "cross")

    def arrive(name):
        received(("cross", name), xs.at[1, :, :, :, :, :, pl.ds(*CHUNKS[name][2])])

    def finish_second(name):
        for split in range(3):
            received(("second", name, split), xref(0, split, 0, slice(1, 4), cols=CHUNKS[name][2]))
            spread(name, split)

    def relayout(name, half):
        first_tile, count, (at, width) = CHUNKS[name]
        for split in range(3):
            span = tiles_of(name, split)
            if span is None:
                continue

            def rows(z, _, split=split, span=span):
                v = xs[half, split, z, :, :, :, at:at + width].astype(F32).reshape(16, 2, 8, width)
                for h in range(2):
                    col = ((half * 2 + h) * count + span[0] - first_tile) * LANE
                    lhs[name][pl.ds(z * 128, 128), col:col + width] = v[:, h].reshape(128, width).astype(BF16)
                return 0

            for z in range(4):
                rows(z, 0)

    def multiply(name, half, begin, end):
        if half == 0 and begin == 0:
            fetched(wgu[name], "ABC".index(name))
        depth = 2 * CHUNKS[name][1] * LANE
        span = slice(half * depth, half * depth + depth)

        def one(i, _):
            product = jnp.dot(lhs[name][:, span], wgu[name][i, span], preferred_element_type=F32)
            if name == "C" and half == 0:
                acc[i] = product
            else:
                acc[i] += product
            return 0

        for i in range(begin, end):
            one(i, 0)

    finish_second("C")
    cross_near("C")
    finish_second("A")
    pass_on("C")
    finish_second("B")
    cross_near("A")
    pass_on("A")
    cross_far("C")
    relayout("C", 0)
    multiply("C", 0, 0, 2)
    arrive("C")
    relayout("C", 1)
    multiply("C", 1, 0, 2)
    pass_on("B")
    cross_far("A")
    cross_near("B")
    relayout("A", 0)
    multiply("A", 0, 0, 2)
    arrive("A")
    relayout("A", 1)
    multiply("A", 1, 0, 1)
    cross_far("B")
    multiply("A", 1, 1, 2)
    relayout("B", 0)
    multiply("B", 0, 0, 2)
    arrive("B")
    relayout("B", 1)
    multiply("B", 1, 0, 2)

    lane = lax.broadcasted_iota(jnp.int32, (128, LANE), 1)

    def weigh(z, _):
        v = xs[0, 2, z, :, :, :, 512:640].astype(F32).reshape(16, 2, 8, LANE)[:, 0].reshape(128, LANE)
        for e in range(2):
            w = jnp.sum(jnp.where(lane % 32 == node * 2 + e, v, 0.0), axis=1, keepdims=True)
            scale[e, pl.ds(z * 128, 128), :] = jnp.broadcast_to(w, (128, 256))
        return 0

    for z in range(4):
        weigh(z, 0)

    def activate(i, _):
        rows = pl.ds(i * 128, 128)
        for e in range(2):
            gate = acc[e, rows, :256]
            hid[e, rows, :] = (gate / (1.0 + jnp.exp(-gate)) * acc[e, rows, 256:]).astype(BF16)
        return 0

    for i in range(4):
        activate(i, 0)

    fetched(wd, 3)

    def project(name, half, target, pairs):
        first_tile, count, (at, width) = CHUNKS[name]
        for pair in pairs:
            lo = (first_tile + 2 * pair) * LANE

            halves = []
            for h in range(2):
                cols = slice(h * QUARTER + lo, h * QUARTER + lo + 256)
                y = scale[0] * jnp.dot(hid[0], wd[half, 0, :, cols], preferred_element_type=F32)
                y = y + scale[1] * jnp.dot(hid[1], wd[half, 1, :, cols], preferred_element_type=F32)
                halves.append(y.reshape(64, 8, 256))
            block = jnp.concatenate(halves, axis=1).astype(BF16).reshape(4, 4, 4, 16, 256)
            if name == "C":
                target[0, :, :, :, :, at:at + width] = block[..., :LANE]
                target[1, :, :, :, :, at:at + width] = block[..., LANE:]
            else:
                target[pair, :, :, :, :, at:at + width] = block

    def splits_of(name):
        return (0, 1) if name == "C" else (0, 1, 2)

    def ref_of(array, name, index):
        return array.at[index + (slice(None), pl.ds(*CHUNKS[name][2]))]

    def produce_other(name, pair=0):
        project(name, 1, other_sum, (pair,))
        for split in (splits_of(name) if name == "C" else (pair,)):
            send(ref_of(other_sum, name, (split,) + place(split)), ref_of(core_got, name, (split,) + place(split)), "core", 0,
                 ("swap", name, split), ("swap", name))

    def produce_own(name, pair=0):
        project(name, 0, own_sum, (pair,))

    def group(array, name, index=()):
        some = slice(0, len(splits_of(name)))
        return array.at[(some,) + index + (slice(None),) * (len(array.shape) - len(index) - 2) + (pl.ds(*CHUNKS[name][2]),)]

    def add(name, target, extras):
        cols = pl.ds(*CHUNKS[name][2])
        total = target[0][target[1] + (slice(None), cols)].astype(F32)
        for array, index in extras:
            total = total + array[index + (slice(None), cols)].astype(F32)
        target[0][target[1] + (slice(None), cols)] = total.astype(BF16)

    def reduce_cores(name, splits):
        for split in splits:
            received(("swap", name, split), ref_of(core_got, name, (split,) + place(split)))

            def slab(z, _, split=split):
                add(name, (own_sum, (split, z, slice(None), slice(None))), [(core_got, (split, z, slice(None), slice(None)))])
                return 0

            for z in range(4):
                slab(z, 0)
            axis = ORDERS[split][2]
            if name == "C":
                for side, step, array, index in ((FAR, 2, r1, (split,)), (FORWARD, 1, r2, (split, 0)), (BACK, 3, r2, (split, 1))):
                    key = "far" if side == FAR else "sides"
                    send(ref_of(own_sum, name, (split,) + place(split, side)), ref_of(array, name, index + plane(split)),
                         axis, step, (key, name, split), (key, name))
                continue
            for part, step in ((lower, 1), (upper, 3)):
                send(ref_of(own_sum, name, (split,) + place(split, FAR, part)), ref_of(r1, name, (split,) + plane(split, part)),
                     axis, step, ("far", step, name, split), ("far", name))
            for side, part, step, way in ((FORWARD, upper, 1, 0), (BACK, lower, 3, 1)):
                send(ref_of(own_sum, name, (split,) + place(split, side, part)),
                     ref_of(r2, name, (split, way) + plane(split, part)), axis, step, ("sides", name, split), ("sides", name))

    def reduce_far(name):
        for split in splits_of(name):
            axis = ORDERS[split][2]
            for side, part, step, way in ((FORWARD, lower, 1, 0), (BACK, upper, 3, 1)):
                received(("far", step, name, split), ref_of(r1, name, (split,) + plane(split, part)))
                add(name, (own_sum, (split,) + place(split, side, part)), [(r1, (split,) + plane(split, part))])
                send(ref_of(own_sum, name, (split,) + place(split, side, part)),
                     ref_of(r2, name, (split, way) + plane(split, part)), axis, step, ("sides", name, split), ("sides", name))

    def reduce_plane(name):
        for split in splits_of(name):
            received(("sides", name, split), ref_of(r2, name, (split,) + (slice(None),) * 3))
            parts = [(r2, (split, 0) + plane(split)), (r2, (split, 1) + plane(split))]
            if name == "C":
                received(("far", name, split), ref_of(r1, name, (split,) + plane(split)))
                parts.append((r1, (split,) + plane(split)))
            add(name, (own_sum, (split,) + place(split, 0)), parts)
            for step in (1, 3, 2):
                send(ref_of(own_sum, name, (split,) + place(split, 0, step)), ref_of(r3, name, (split, step, slice(None))),
                     ORDERS[split][1], step, ("row", name, split), ("row", name))

    def reduce_row(name):
        for split in splits_of(name):
            received(("row", name, split), ref_of(r3, name, (split, slice(1, 4), slice(None))))
            add(name, (own_sum, (split,) + place(split, 0, 0)), [(r3, (split, step, slice(None))) for step in (1, 2, 3)])
            for step in (1, 3, 2):
                send(ref_of(own_sum, name, (split,) + place(split, 0, 0, step)), ref_of(r4, name, (split, step)),
                     ORDERS[split][0], step, ("one", name), ("one", name))

    def reduce_last(name):
        cols = pl.ds(*CHUNKS[name][2])
        received(("one", name), group(r4, name, (slice(1, 4),)))
        for split in splits_of(name):
            total = own_sum[split, 0, 0, 0, :, cols].astype(F32)
            for step in (1, 2, 3):
                total = total + r4[split, step, :, cols].astype(F32)
            fin[split, :, cols] = total.astype(BF16)

    for split in range(3):
        produce_other("A", split)
    for split in range(3):
        produce_own("A", split)
        reduce_cores("A", (split,))
    for split in range(3):
        produce_other("B", split)
    produce_other("C")
    for split in range(3):
        produce_own("B", split)
        reduce_cores("B", (split,))
    produce_own("C")
    reduce_far("A")
    reduce_cores("C", (0, 1))
    reduce_far("B")
    reduce_plane("A")
    reduce_plane("B")
    reduce_plane("C")
    reduce_row("A")
    reduce_row("B")
    reduce_row("C")
    for name in "ABC":
        reduce_last(name)

    send(fin, fin_got, "core", 0, "last", "last")
    received("last", fin_got)
    for split in range(3):
        for name, (_, _, (at, width)) in CHUNKS.items():
            span = tiles_of(name, split)
            if span is None:
                continue
            a = fin[split, :, at:at + width].astype(F32)
            b = fin_got[split, :, at:at + width].astype(F32)
            for half in range(2):
                v = jnp.where(core == half, a, b)
                for h in range(2):
                    col = half * HALF + h * QUARTER + span[0] * LANE
                    rows = jnp.where(core == 0, v[8 * h:8 * h + 4], v[8 * h + 4:8 * h + 8])
                    out[:, col:col + width] = rows.astype(BF16)
    all_sent("entry", got)
    all_sent("first", xs.at[0, :, 0, 0, 1:4])
    all_sent("second", xs.at[0, :, 0, 1:4])
    all_sent("third", xs.at[0, :, 1:3])
    all_sent("passed", xs.at[0, :, 1])
    all_sent("cross", xs.at[1])
    for name in CHUNKS:
        all_sent(("swap", name), group(core_got, name))
        all_sent(("far", name), group(r1, name))
        all_sent(("sides", name), group(r2, name))
        all_sent(("row", name), group(r3, name, (slice(1, 4),)))
        all_sent(("one", name), group(r4, name, (slice(1, 4),)))
    all_sent("last", fin_got)


def on_device(tokens, expert_ids, route_weights, w_gate, w_up, w_down):
    vmem = pl.BlockSpec(memory_space=pltpu.VMEM)
    anywhere = pl.BlockSpec(memory_space=pl.ANY)
    grid3 = (3, 4, 4, 4, 16, WIDE)
    return pl.pallas_call(
        kernel,
        out_shape=jax.ShapeDtypeStruct((4, 7168), BF16),
        in_specs=[vmem, vmem, vmem, anywhere, anywhere, anywhere],
        out_specs=vmem,
        scratch_shapes=[
            pltpu.VMEM((8, HALF + LANE), F32),
            pltpu.VMEM((8, HALF + LANE), F32),
            pltpu.VMEM((8, HALF + LANE), F32),
            pltpu.VMEM((2,) + grid3, BF16),
            pltpu.VMEM((TOKENS, 24 * LANE), BF16),
            pltpu.VMEM((TOKENS, 24 * LANE), BF16),
            pltpu.VMEM((TOKENS, 8 * LANE), BF16),
            pltpu.VMEM((2, 24 * LANE, 512), BF16),
            pltpu.VMEM((2, 24 * LANE, 512), BF16),
            pltpu.VMEM((2, 8 * LANE, 512), BF16),
            pltpu.VMEM((2, 2, 256, HALF), BF16),
            pltpu.VMEM((2, TOKENS, 512), F32),
            pltpu.VMEM((2, TOKENS, 256), BF16),
            pltpu.VMEM((2, TOKENS, 256), F32),
            pltpu.VMEM(grid3, BF16),
            pltpu.VMEM(grid3, BF16),
            pltpu.VMEM(grid3, BF16),
            pltpu.VMEM((3, 4, 4, 16, WIDE), BF16),
            pltpu.VMEM((3, 2, 4, 4, 16, WIDE), BF16),
            pltpu.VMEM((3, 4, 4, 16, WIDE), BF16),
            pltpu.VMEM((3, 4, 16, WIDE), BF16),
            pltpu.VMEM((3, 16, WIDE), BF16),
            pltpu.VMEM((3, 16, WIDE), BF16),
            pltpu.SemaphoreType.DMA((N_SEND,)),
            pltpu.SemaphoreType.DMA((N_RECV,)),
            pltpu.SemaphoreType.DMA((4,)),
        ],
        compiler_params=pltpu.CompilerParams(
            collective_id=0, has_side_effects=True, vmem_limit_bytes=62 * 2**20),
        cost_estimate=pl.CostEstimate(flops=11_300_000_000, bytes_accessed=22_100_000, transcendentals=262_144),
    )(tokens, expert_ids, route_weights, w_gate, w_up, w_down)


def solution(mesh):
    placed = (
        P(("node", "local"), None),
        P(("node", "local"), None),
        P(("node", "local"), None),
        P("node", None, "local"),
        P("node", None, "local"),
        P("node", "local", None),
    )
    return jax.shard_map(
        on_device, mesh=mesh, in_specs=placed, out_specs=P(("node", "local"), None), check_vma=False
    )
```

```python
import jax
import jax.numpy as jnp
from jax import lax
from jax.experimental import pallas as pl
from jax.experimental.pallas import tpu as pltpu
from jax.sharding import PartitionSpec as P

MESH = pl.DeviceIdType.MESH
F32, BF16 = jnp.float32, jnp.bfloat16
LANE = 128
HALF = 3584
QUARTER = 1792
TOKENS = 512
WIDE = 640
ORDERS = ("xyz", "yzx", "zxy")
PLACE = {"z": 0, "y": 1, "x": 2}
FORWARD, BACK, FAR = 1, 3, 2
CHUNKS = {"A": (0, 6, (0, 256)), "B": (6, 6, (256, 256)), "C": (12, 2, (512, 128))}
N_SEND, N_RECV = 22, 85


def coordinates():
    node, local = lax.axis_index("node"), lax.axis_index("local")
    return {"x": local // 2, "y": node // 4, "z": node % 4, "core": local % 2}


def neighbour(axis, step):
    at = coordinates()
    if axis == "core":
        at["core"] = 1 - at["core"]
    else:
        at[axis] = lax.rem(at[axis] + step, 4)
    return (at["y"] * 4 + at["z"], at["x"] * 2 + at["core"])


def place(split, c=slice(None), b=slice(None), a=slice(None)):
    order = ORDERS[split]
    index = [None, None, None]
    for axis, value in zip(order, (a, b, c)):
        index[PLACE[axis]] = value
    return tuple(index)


def plane(split, b=slice(None), a=slice(None)):
    order = ORDERS[split]
    return tuple(v for _, v in sorted([(PLACE[order[0]], a), (PLACE[order[1]], b)], key=lambda p: p[0]))


def tiles_of(chunk, split):
    first, count, _ = CHUNKS[chunk]
    if chunk == "C":
        return (first + split, 1) if split < 2 else None
    return (first + 2 * split, 2)


def kernel(tokens, ids, weights, w_gate, w_up, w_down, out,
           own, sent, got, xs, lhs_a, lhs_b, lhs_c, wgu_a, wgu_b, wgu_c, wd, acc, hid, scale,
           own_sum, other_sum, core_got, r1, r2, r3, r4, fin, fin_got, send_sem, recv_sem, local_sem):
    core = lax.axis_index("local") % 2
    node = lax.axis_index("node")
    send_slots, recv_slots, send_totals = {}, {}, {}

    def slot(table, key):
        return table.setdefault(key, len(table))

    def send(src, dst, axis, step, recv_key, send_key):
        copy = pltpu.make_async_remote_copy(
            src_ref=src, dst_ref=dst, send_sem=send_sem.at[slot(send_slots, send_key)],
            recv_sem=recv_sem.at[slot(recv_slots, recv_key)],
            device_id=neighbour(axis, step), device_id_type=MESH)
        copy.start()

    def received(key, ref):
        pltpu.make_async_copy(ref, ref, recv_sem.at[recv_slots[key]]).wait()

    def all_sent(key, ref):
        pltpu.make_async_copy(ref, ref, send_sem.at[send_slots[key]]).wait()

    barrier = pltpu.get_barrier_semaphore()
    friends = [(axis, step) for axis in "xyz" for step in (1, 2, 3)] + [("core", 0)]
    for axis, step in friends:
        pl.semaphore_signal(barrier, inc=1, device_id=neighbour(axis, step), device_id_type=MESH)

    def fetch(src, dst, i):
        pltpu.make_async_copy(src, dst, local_sem.at[i]).start()

    def fetched(ref, i):
        pltpu.make_async_copy(ref, ref, local_sem.at[i]).wait()

    wgu = {"A": wgu_a, "B": wgu_b, "C": wgu_c}
    lhs = {"A": lhs_a, "B": lhs_b, "C": lhs_c}

    def fetch_chunk(name):
        first, count, _ = CHUNKS[name]
        for which, source in enumerate((w_gate, w_up)):
            for half in range(2):
                side = lax.rem(core + half, 2)
                for h in range(2):
                    start = pl.multiple_of(side * HALF + h * QUARTER + first * LANE, LANE)
                    fetch(source.at[:, pl.ds(start, count * LANE), :],
                          wgu[name].at[:, pl.ds((half * 2 + h) * count * LANE, count * LANE), 256 * which:256 * which + 256], "ABC".index(name))

    fetch_chunk("A")

    row4 = lax.broadcasted_iota(jnp.int32, (4, LANE), 1)
    dense = jnp.zeros((4, LANE), F32)
    for k in range(8):
        dense = dense + jnp.where(row4 % 32 == ids[:, k:k + 1], weights[:, k:k + 1], 0.0)
    high = dense.astype(BF16).astype(F32)
    mid = (dense - high).astype(BF16).astype(F32)
    low = dense - high - mid
    meta = jnp.where(row4 < 32, high, jnp.where(row4 < 64, mid, jnp.where(row4 < 96, low, 0.0)))
    left = tokens[:, :HALF].astype(F32)
    right = tokens[:, HALF:].astype(F32)
    mine = jnp.where(core == 0, left, right)
    theirs = jnp.where(core == 0, right, left)
    for r in (0, 4):
        own[r:r + 4, :HALF] = mine
        own[r:r + 4, HALF:] = meta
        sent[r:r + 4, :HALF] = theirs
        sent[r:r + 4, HALF:] = meta

    pl.semaphore_wait(barrier, len(friends))

    send(sent, got, "core", 0, "entry", "entry")
    fetch_chunk("B")
    received("entry", got)
    block = jnp.where(lax.broadcasted_iota(jnp.int32, (8, HALF + LANE), 0) // 4 == core, own[...], got[...])
    for split in range(3):
        for name, (_, _, (at, width)) in CHUNKS.items():
            span = tiles_of(name, split)
            if span is None:
                piece = jnp.concatenate([block[:, HALF:], block[:, HALF:]], axis=0)
            else:
                lo = span[0] * LANE
                piece = jnp.concatenate([block[:, lo:lo + width], block[:, QUARTER + lo:QUARTER + lo + width]], axis=0)
            xs[0, split, 0, 0, 0, :, at:at + width] = piece.astype(BF16)

    def xref(half, split, c, b=slice(None), a=slice(None), cols=None):
        index = (half, split) + place(split, c, b, a)
        if cols is not None:
            index = index + (slice(None), pl.ds(*cols))
        return xs.at[index]

    for split in range(3):
        for step in (1, 3, 2):
            send(xref(0, split, 0, 0, 0), xref(0, split, 0, 0, (4 - step) % 4), ORDERS[split][0], step, ("first", split), "first")
    fetch_chunk("C")
    for half in range(2):
        side = lax.rem(core + half, 2)
        fetch(w_down.at[:, :, pl.ds(pl.multiple_of(side * HALF, LANE), HALF)], wd.at[half], 3)
    for split in range(3):
        received(("first", split), xref(0, split, 0, 0, slice(1, 4)))
        for name in "CAB":
            cols = CHUNKS[name][2]
            for step in (1, 3, 2):
                send(xref(0, split, 0, 0, cols=cols), xref(0, split, 0, (4 - step) % 4, cols=cols), ORDERS[split][1], step,
                     ("second", name, split), "second")

    lower, upper = slice(0, 2), slice(2, 4)

    def spread(name, split):
        cols = CHUNKS[name][2]
        axis = ORDERS[split][2]
        send(xref(0, split, 0, cols=cols), xref(0, split, BACK, cols=cols), axis, 1, ("third", BACK, name, split), "third")
        send(xref(0, split, 0, cols=cols), xref(0, split, FORWARD, cols=cols), axis, 3, ("third", FORWARD, name, split), "third")

    def pass_on(name):
        cols = CHUNKS[name][2]
        for split in range(3):
            axis = ORDERS[split][2]
            for side, part, step in ((BACK, lower, 1), (FORWARD, upper, 3)):
                received(("third", side, name, split), xref(0, split, side, cols=cols))
                send(xref(0, split, side, part, cols=cols), xref(0, split, FAR, part, cols=cols), axis, step,
                     ("passed", name, split), "passed")
                send(xref(0, split, side, cols=cols), xref(1, split, side, cols=cols), "core", 0, ("cross", name), "cross")

    def cross_far(name):
        cols = CHUNKS[name][2]
        for split in range(3):
            received(("passed", name, split), xref(0, split, FAR, cols=cols))
            send(xref(0, split, FAR, cols=cols), xref(1, split, FAR, cols=cols), "core", 0, ("cross", name), "cross")

    def cross_near(name):
        cols = CHUNKS[name][2]
        for split in range(3):
            send(xref(0, split, 0, cols=cols), xref(1, split, 0, cols=cols), "core", 0, ("cross", name), "cross")

    def arrive(name):
        received(("cross", name), xs.at[1, :, :, :, :, :, pl.ds(*CHUNKS[name][2])])

    def finish_second(name):
        for split in range(3):
            received(("second", name, split), xref(0, split, 0, slice(1, 4), cols=CHUNKS[name][2]))
            spread(name, split)

    def relayout(name, half):
        first_tile, count, (at, width) = CHUNKS[name]
        for split in range(3):
            span = tiles_of(name, split)
            if span is None:
                continue

            def rows(z, _, split=split, span=span):
                v = xs[half, split, z, :, :, :, at:at + width].astype(F32).reshape(16, 2, 8, width)
                for h in range(2):
                    col = ((half * 2 + h) * count + span[0] - first_tile) * LANE
                    lhs[name][pl.ds(z * 128, 128), col:col + width] = v[:, h].reshape(128, width).astype(BF16)
                return 0

            for z in range(4):
                rows(z, 0)

    def multiply(name, half, begin, end):
        if half == 0 and begin == 0:
            fetched(wgu[name], "ABC".index(name))
        depth = 2 * CHUNKS[name][1] * LANE
        span = slice(half * depth, half * depth + depth)

        def one(i, _):
            product = jnp.dot(lhs[name][:, span], wgu[name][i, span], preferred_element_type=F32)
            if name == "C" and half == 0:
                acc[i] = product
            else:
                acc[i] += product
            return 0

        for i in range(begin, end):
            one(i, 0)

    finish_second("C")
    cross_near("C")
    finish_second("A")
    pass_on("C")
    finish_second("B")
    cross_near("A")
    pass_on("A")
    cross_far("C")
    relayout("C", 0)
    multiply("C", 0, 0, 2)
    arrive("C")
    relayout("C", 1)
    multiply("C", 1, 0, 2)

    lane = lax.broadcasted_iota(jnp.int32, (128, LANE), 1)

    def weigh(z, _):
        v = xs[0, 2, z, :, :, :, 512:640].astype(F32).reshape(16, 2, 8, LANE)[:, 0].reshape(128, LANE)
        for e in range(2):
            w = jnp.sum(jnp.where(lane % 32 == node * 2 + e, v, 0.0), axis=1, keepdims=True)
            scale[e, pl.ds(z * 128, 128), :] = jnp.broadcast_to(w, (128, 256))
        return 0

    for z in range(4):
        weigh(z, 0)

    pass_on("B")
    cross_far("A")
    cross_near("B")
    relayout("A", 0)
    multiply("A", 0, 0, 2)
    arrive("A")
    relayout("A", 1)
    multiply("A", 1, 0, 1)
    cross_far("B")
    multiply("A", 1, 1, 2)
    relayout("B", 0)
    multiply("B", 0, 0, 2)
    arrive("B")
    relayout("B", 1)
    multiply("B", 1, 0, 2)

    def activate(i, _):
        rows = pl.ds(i * 128, 128)
        for e in range(2):
            gate = acc[e, rows, :256]
            hid[e, rows, :] = (gate / (1.0 + jnp.exp(-gate)) * acc[e, rows, 256:]).astype(BF16)
        return 0

    for i in range(4):
        activate(i, 0)

    fetched(wd, 3)

    def project(name, half, target, pairs):
        first_tile, count, (at, width) = CHUNKS[name]
        for pair in pairs:
            lo = (first_tile + 2 * pair) * LANE

            halves = []
            for h in range(2):
                cols = slice(h * QUARTER + lo, h * QUARTER + lo + 256)
                y = scale[0] * jnp.dot(hid[0], wd[half, 0, :, cols], preferred_element_type=F32)
                y = y + scale[1] * jnp.dot(hid[1], wd[half, 1, :, cols], preferred_element_type=F32)
                halves.append(y.reshape(64, 8, 256))
            block = jnp.concatenate(halves, axis=1).astype(BF16).reshape(4, 4, 4, 16, 256)
            if name == "C":
                target[0, :, :, :, :, at:at + width] = block[..., :LANE]
                target[1, :, :, :, :, at:at + width] = block[..., LANE:]
            else:
                target[pair, :, :, :, :, at:at + width] = block

    def splits_of(name):
        return (0, 1) if name == "C" else (0, 1, 2)

    def ref_of(array, name, index):
        return array.at[index + (slice(None), pl.ds(*CHUNKS[name][2]))]

    def produce_other(name, pair=0):
        project(name, 1, other_sum, (pair,))
        for split in (splits_of(name) if name == "C" else (pair,)):
            send(ref_of(other_sum, name, (split,) + place(split)), ref_of(core_got, name, (split,) + place(split)), "core", 0,
                 ("swap", name, split), ("swap", name))

    def produce_own(name, pair=0):
        project(name, 0, own_sum, (pair,))

    def group(array, name, index=()):
        some = slice(0, len(splits_of(name)))
        return array.at[(some,) + index + (slice(None),) * (len(array.shape) - len(index) - 2) + (pl.ds(*CHUNKS[name][2]),)]

    def add(name, target, extras):
        cols = pl.ds(*CHUNKS[name][2])
        total = target[0][target[1] + (slice(None), cols)].astype(F32)
        for array, index in extras:
            total = total + array[index + (slice(None), cols)].astype(F32)
        target[0][target[1] + (slice(None), cols)] = total.astype(BF16)

    def reduce_cores(name, splits):
        for split in splits:
            received(("swap", name, split), ref_of(core_got, name, (split,) + place(split)))

            def slab(z, _, split=split):
                add(name, (own_sum, (split, z, slice(None), slice(None))), [(core_got, (split, z, slice(None), slice(None)))])
                return 0

            for z in range(4):
                slab(z, 0)
            axis = ORDERS[split][2]
            if name == "C":
                for side, step, array, index in ((FAR, 2, r1, (split,)), (FORWARD, 1, r2, (split, 0)), (BACK, 3, r2, (split, 1))):
                    key = "far" if side == FAR else "sides"
                    send(ref_of(own_sum, name, (split,) + place(split, side)), ref_of(array, name, index + plane(split)),
                         axis, step, (key, name, split), (key, name))
                continue
            for part, step in ((lower, 1), (upper, 3)):
                send(ref_of(own_sum, name, (split,) + place(split, FAR, part)), ref_of(r1, name, (split,) + plane(split, part)),
                     axis, step, ("far", step, name, split), ("far", name))
            for side, part, step, way in ((FORWARD, upper, 1, 0), (BACK, lower, 3, 1)):
                send(ref_of(own_sum, name, (split,) + place(split, side, part)),
                     ref_of(r2, name, (split, way) + plane(split, part)), axis, step, ("sides", name, split), ("sides", name))

    def reduce_far(name):
        for split in splits_of(name):
            axis = ORDERS[split][2]
            for side, part, step, way in ((FORWARD, lower, 1, 0), (BACK, upper, 3, 1)):
                received(("far", step, name, split), ref_of(r1, name, (split,) + plane(split, part)))
                add(name, (own_sum, (split,) + place(split, side, part)), [(r1, (split,) + plane(split, part))])
                send(ref_of(own_sum, name, (split,) + place(split, side, part)),
                     ref_of(r2, name, (split, way) + plane(split, part)), axis, step, ("sides", name, split), ("sides", name))

    def reduce_plane(name):
        for split in splits_of(name):
            received(("sides", name, split), ref_of(r2, name, (split,) + (slice(None),) * 3))
            parts = [(r2, (split, 0) + plane(split)), (r2, (split, 1) + plane(split))]
            if name == "C":
                received(("far", name, split), ref_of(r1, name, (split,) + plane(split)))
                parts.append((r1, (split,) + plane(split)))
            add(name, (own_sum, (split,) + place(split, 0)), parts)
            for step in (1, 3, 2):
                send(ref_of(own_sum, name, (split,) + place(split, 0, step)), ref_of(r3, name, (split, step, slice(None))),
                     ORDERS[split][1], step, ("row", name, split), ("row", name))

    def reduce_row(name):
        for split in splits_of(name):
            received(("row", name, split), ref_of(r3, name, (split, slice(1, 4), slice(None))))
            add(name, (own_sum, (split,) + place(split, 0, 0)), [(r3, (split, step, slice(None))) for step in (1, 2, 3)])
            for step in (1, 3, 2):
                send(ref_of(own_sum, name, (split,) + place(split, 0, 0, step)), ref_of(r4, name, (split, step)),
                     ORDERS[split][0], step, ("one", name), ("one", name))

    def reduce_last(name):
        cols = pl.ds(*CHUNKS[name][2])
        received(("one", name), group(r4, name, (slice(1, 4),)))
        for split in splits_of(name):
            total = own_sum[split, 0, 0, 0, :, cols].astype(F32)
            for step in (1, 2, 3):
                total = total + r4[split, step, :, cols].astype(F32)
            fin[split, :, cols] = total.astype(BF16)

    for split in range(3):
        produce_other("A", split)
    for split in range(3):
        produce_own("A", split)
        reduce_cores("A", (split,))
    for split in range(3):
        produce_other("B", split)
    produce_other("C")
    for split in range(3):
        produce_own("B", split)
        reduce_cores("B", (split,))
    produce_own("C")
    reduce_far("A")
    reduce_cores("C", (0, 1))
    reduce_far("B")
    reduce_plane("A")
    reduce_plane("B")
    reduce_plane("C")
    reduce_row("A")
    reduce_row("B")
    reduce_row("C")
    for name in "ABC":
        reduce_last(name)

    send(fin, fin_got, "core", 0, "last", "last")
    received("last", fin_got)
    for split in range(3):
        for name, (_, _, (at, width)) in CHUNKS.items():
            span = tiles_of(name, split)
            if span is None:
                continue
            a = fin[split, :, at:at + width].astype(F32)
            b = fin_got[split, :, at:at + width].astype(F32)
            for half in range(2):
                v = jnp.where(core == half, a, b)
                for h in range(2):
                    col = half * HALF + h * QUARTER + span[0] * LANE
                    rows = jnp.where(core == 0, v[8 * h:8 * h + 4], v[8 * h + 4:8 * h + 8])
                    out[:, col:col + width] = rows.astype(BF16)
    all_sent("entry", got)
    all_sent("first", xs.at[0, :, 0, 0, 1:4])
    all_sent("second", xs.at[0, :, 0, 1:4])
    all_sent("third", xs.at[0, :, 1:3])
    all_sent("passed", xs.at[0, :, 1])
    all_sent("cross", xs.at[1])
    for name in CHUNKS:
        all_sent(("swap", name), group(core_got, name))
        all_sent(("far", name), group(r1, name))
        all_sent(("sides", name), group(r2, name))
        all_sent(("row", name), group(r3, name, (slice(1, 4),)))
        all_sent(("one", name), group(r4, name, (slice(1, 4),)))
    all_sent("last", fin_got)


def on_device(tokens, expert_ids, route_weights, w_gate, w_up, w_down):
    vmem = pl.BlockSpec(memory_space=pltpu.VMEM)
    anywhere = pl.BlockSpec(memory_space=pl.ANY)
    grid3 = (3, 4, 4, 4, 16, WIDE)
    return pl.pallas_call(
        kernel,
        out_shape=jax.ShapeDtypeStruct((4, 7168), BF16),
        in_specs=[vmem, vmem, vmem, anywhere, anywhere, anywhere],
        out_specs=vmem,
        scratch_shapes=[
            pltpu.VMEM((8, HALF + LANE), F32),
            pltpu.VMEM((8, HALF + LANE), F32),
            pltpu.VMEM((8, HALF + LANE), F32),
            pltpu.VMEM((2,) + grid3, BF16),
            pltpu.VMEM((TOKENS, 24 * LANE), BF16),
            pltpu.VMEM((TOKENS, 24 * LANE), BF16),
            pltpu.VMEM((TOKENS, 8 * LANE), BF16),
            pltpu.VMEM((2, 24 * LANE, 512), BF16),
            pltpu.VMEM((2, 24 * LANE, 512), BF16),
            pltpu.VMEM((2, 8 * LANE, 512), BF16),
            pltpu.VMEM((2, 2, 256, HALF), BF16),
            pltpu.VMEM((2, TOKENS, 512), F32),
            pltpu.VMEM((2, TOKENS, 256), BF16),
            pltpu.VMEM((2, TOKENS, 256), F32),
            pltpu.VMEM(grid3, BF16),
            pltpu.VMEM(grid3, BF16),
            pltpu.VMEM(grid3, BF16),
            pltpu.VMEM((3, 4, 4, 16, WIDE), BF16),
            pltpu.VMEM((3, 2, 4, 4, 16, WIDE), BF16),
            pltpu.VMEM((3, 4, 4, 16, WIDE), BF16),
            pltpu.VMEM((3, 4, 16, WIDE), BF16),
            pltpu.VMEM((3, 16, WIDE), BF16),
            pltpu.VMEM((3, 16, WIDE), BF16),
            pltpu.SemaphoreType.DMA((N_SEND,)),
            pltpu.SemaphoreType.DMA((N_RECV,)),
            pltpu.SemaphoreType.DMA((4,)),
        ],
        compiler_params=pltpu.CompilerParams(
            collective_id=0, has_side_effects=True, vmem_limit_bytes=62 * 2**20),
        cost_estimate=pl.CostEstimate(flops=11_300_000_000, bytes_accessed=22_100_000, transcendentals=262_144),
    )(tokens, expert_ids, route_weights, w_gate, w_up, w_down)


def solution(mesh):
    placed = (
        P(("node", "local"), None),
        P(("node", "local"), None),
        P(("node", "local"), None),
        P("node", None, "local"),
        P("node", None, "local"),
        P("node", "local", None),
    )
    return jax.shard_map(
        on_device, mesh=mesh, in_specs=placed, out_specs=P(("node", "local"), None), check_vma=False
    )
```
